32 devices in a mesh: groups: 2 (over y), queue: 4 (over z), dp: 4 (over x, core).
Axes of the slice: x: 2, y: 2, z: 4, core: 2. Of those that a mesh axis runs over, the one named last changes fastest.
Arguments:
- query_inputs: bfloat16 [8192, 1024], P(('groups', 'queue', 'dp')), parts along dimension 0, may hold values from -30 to 30
- key_inputs: bfloat16 [512, 1024], P(('groups', 'queue', 'dp')), parts along dimension 0, may hold values from -6 to 6
- query_weight: bfloat16 [1024, 1024], replicated, may hold values from -4 to 4
- key_weight: bfloat16 [1024, 1024], replicated, may hold values from -0.1875 to 0.1875
- queue_keys: bfloat16 [2048, 1024], P(('groups', 'queue')), parts along dimension 0, may hold values from -2 to 2
- write_pointer: int32 [2], P('groups'), parts along dimension 0, may hold values from 0 to 255
- slot_owner: int32 [32], P('groups'), parts along dimension 0, may hold values from 0 to 15, each once
- positive_index: int32 [8192], P(('groups', 'queue', 'dp')), parts along dimension 0, may hold values from 0 to 1023
Outputs:
- loss: float32 [8192], P(('groups', 'queue', 'dp')), parts along dimension 0
- query_weight_grad: float32 [2048, 1024], P(('groups', 'queue', 'dp')), parts along dimension 0
- new_queue: bfloat16 [2048, 1024], P(('groups', 'queue')), parts along dimension 0
The draws below stay inside these ranges and needn't reach their ends.
There are 2 independent parts, one for each index of `groups`. The reference program is written for one: setup_inputs(seed, part) draws one part's arguments, and reference() takes and returns one part's arrays. A program takes and returns all parts, laid end to end along the dimension named above; an argument that names none is the same for every part. Nothing has to cross between parts.
Inputs may be any that keep to these rules, and one draw needn't show every extreme that they name: slot_owner is a permutation of 0 to 15.
All inputs are finite; a program needn't handle non-finite values.
Results may differ from the reference program's by a relative error of at most 0.0075.
Values may be sent and summed in bfloat16 or wider, within the bound.
A program may use at most 192 MiB of HBM per device.

```python
import math
import jax
import jax.numpy as jnp
from jax import lax

D = 1024
Q_DEV = 256
K_DEV = 256
NEW_DEV = 16
QUERIES = 4096
KEYS = 1024
BLOCKS = 16
NEWKEYS = 256
N_QUEUE = 4
N_DP = 4


def draw_queue_keys(key, part):
    key_entries = jax.random.fold_in(key, 11)
    spread = D ** (-0.5)
    entries = jnp.clip(jax.random.normal(key_entries, (KEYS, D), jnp.float32), -6.0, 6.0) * spread
    return entries.astype(jnp.bfloat16)


def draw_query_inputs(key, part):
    key_entries = jax.random.fold_in(key, 13)
    group_count = N_QUEUE * N_DP
    pairing = jax.random.permutation(jax.random.fold_in(key, 17), group_count)
    row_index = jnp.arange(QUERIES, dtype=jnp.int32)
    column_index = jnp.arange(D, dtype=jnp.int32)
    column_block = column_index // (D // group_count)
    row_pair = pairing[row_index // Q_DEV]
    spike_gain = jnp.where(row_pair[:, None] == column_block[None, :], 4.0, 1.0)
    entries = jnp.clip(jax.random.normal(key_entries, (QUERIES, D), jnp.float32), -6.0, 6.0) * spike_gain
    return entries.astype(jnp.bfloat16)


def draw_query_weight(key, part):
    key_entries = jax.random.fold_in(key, 19)
    spread = D ** (-0.5)
    entries = jnp.clip(jax.random.normal(key_entries, (D, D), jnp.float32), -6.0, 6.0) * spread
    return entries.astype(jnp.bfloat16)


def with_ends(result, rng, low, high):
    place = [jax.random.randint(jax.random.fold_in(rng, axis), (), 0, length) for axis, length in enumerate(result.shape)]
    longest = result.shape.index(max(result.shape))
    neighbour = place[:longest] + [(place[longest] + 1) % result.shape[longest]] + place[longest + 1:]
    return result.at[tuple(place)].set(low).at[tuple(neighbour)].set(high)


def level_of(rng, shape, shards, smallest, top_value):
    loudness = 1.0
    for dim, parts in shards:
        heights = jax.random.uniform(jax.random.fold_in(jax.random.fold_in(rng, 6), dim), (parts,), jnp.float32, smallest / len(shards), top_value / len(shards))
        loudness = loudness * jnp.repeat(jnp.exp(heights), shape[dim] // parts).reshape((-1,) + (1,) * (len(shape) - 1 - dim))
    return loudness


def normal_values(rng, extent, scale, bound, pieces=(), kind=jnp.bfloat16):
    level = level_of(rng, extent, pieces, -0.22, 0.18) if pieces else 1.0
    result = jax.random.normal(rng, extent, jnp.float32) * scale * level
    return jnp.minimum(jnp.maximum(result, -bound), bound).astype(kind)


def setup_inputs(seed: int = 0, part: int = 0) -> dict:
    key_list = jax.random.split(jax.random.key(seed), 9)
    part_keys = jax.random.split(jax.random.fold_in(key_list[8], part), 9)
    return {
        "query_inputs": draw_query_inputs(jax.random.fold_in(jax.random.fold_in(key_list[8], part), 71), part),
        "key_inputs": normal_values(part_keys[1], (NEWKEYS, D), 1.0, 6.0, ((0, 16),)),
        "query_weight": draw_query_weight(jax.random.fold_in(key_list[8], 71), part),
        "key_weight": normal_values(key_list[3], (D, D), D ** -0.5, 0.1875),
        "queue_keys": draw_queue_keys(jax.random.fold_in(jax.random.fold_in(key_list[8], part), 71), part),
        "write_pointer": jax.random.randint(part_keys[5], (1,), 0, K_DEV).astype(jnp.int32),
        "slot_owner": jax.random.permutation(part_keys[6], BLOCKS).astype(jnp.int32),
        "positive_index": with_ends(jax.random.randint(part_keys[7], (QUERIES,), 0, KEYS), jax.random.fold_in(part_keys[7], 1), 0, KEYS - 1).astype(jnp.int32),
    }


temper = 0.05

def unit_rows(matrix):
    return matrix * lax.rsqrt(lax.optimization_barrier(jnp.sum(matrix * matrix, -1, keepdims=True)) + 1e-06)

def reference(query_inputs, key_inputs, query_weight, key_weight, queue_keys, write_pointer, slot_owner, positive_index):
    query = jnp.dot(query_inputs, query_weight, preferred_element_type=jnp.float32)
    inv_len = lax.rsqrt(lax.optimization_barrier(jnp.sum(query * query, -1, keepdims=True)) + 1e-06)
    unit_f = query * inv_len
    unit = unit_f.astype(jnp.bfloat16)
    width = math.gcd(QUERIES, 2048)

    def one_block(rows):
        scores = jnp.dot(rows, queue_keys.T, preferred_element_type=jnp.float32) / temper
        top = lax.optimization_barrier(jnp.max(scores, -1))
        expo = jnp.exp(scores - top[:, None])
        total = lax.optimization_barrier(jnp.sum(expo, -1))
        mixture = jnp.dot(expo.astype(jnp.bfloat16), queue_keys, preferred_element_type=jnp.float32) / total[:, None]
        return (top, total, mixture)
    top, total, mixture = lax.map(one_block, unit.reshape(QUERIES // width, width, D))
    top = top.reshape(QUERIES)
    total = total.reshape(QUERIES)
    mixture = mixture.reshape(QUERIES, D)
    chosen = jnp.take(queue_keys, positive_index, axis=0).astype(jnp.float32)
    positive = lax.optimization_barrier(jnp.sum(unit.astype(jnp.float32) * chosen, -1)) / temper
    loss = top + jnp.log(total) - positive
    grad_unit = (mixture - chosen) / temper
    grad_query = ((grad_unit - unit_f * lax.optimization_barrier(jnp.sum(unit_f * grad_unit, -1, keepdims=True))) * inv_len).astype(jnp.bfloat16)
    query_weight_grad = jnp.dot(query_inputs.T, grad_query, preferred_element_type=jnp.float32)
    fresh = unit_rows(jnp.dot(key_inputs, key_weight, preferred_element_type=jnp.float32)).astype(jnp.bfloat16)
    rows = jnp.arange(KEYS, dtype=jnp.int32)
    shard = rows // K_DEV
    offset = (rows % K_DEV - write_pointer[0]) % K_DEV
    live = offset < N_DP * NEW_DEV
    slot = shard * N_DP + jnp.minimum(offset // NEW_DEV, N_DP - 1)
    inverse = jnp.zeros((BLOCKS,), jnp.int32).at[slot_owner].set(jnp.arange(BLOCKS, dtype=jnp.int32))
    source = (jnp.take(inverse, slot) * NEW_DEV + offset % NEW_DEV).astype(jnp.int32)
    new_queue = jnp.where(live[:, None], jnp.take(fresh, source, axis=0), queue_keys)
    return (loss, query_weight_grad, new_queue)
```

```python
import functools

import jax
import jax.numpy as jnp
from jax import lax
from jax.experimental import pallas as pl
from jax.experimental.pallas import tpu as pltpu
from jax.sharding import PartitionSpec as P

temper = 0.05
MESH = pl.DeviceIdType.MESH
F32 = jnp.float32
BF16 = jnp.bfloat16


def dot(a, b, da, db):
    return lax.dot_general(a, b, (((da,), (db,)), ((), ())), preferred_element_type=F32)


def kernel(
    nq, nd,
    pointer_ref, owner_ref, index_ref, x_hbm, kin_hbm, wq_hbm, wk_hbm, keys_hbm,
    loss_ref, grad_ref, queue_ref,
    x_ref, kin_ref, wq_ref, wk_ref, keys, fresh,
    unit_f, unit, inv_len, top, total, posit, pos_col, mixture, chosen,
    xt, grad_q, core_out, core_in, part, x_out, x_in, up_in, down_in, z_out,
    load_sem, up_send, down_send, z_recv, x_send, x_recv, c_send, c_recv,
    fz_send, fz_recv, f_send, f_recv,
    gc_send, gc_recv, gx_send, gx_recv, gu_send, gd_send, gu_recv, gd_recv,
):
    q = lax.axis_index("queue")
    d = lax.axis_index("dp")
    hi, lo = d // 2, d % 2
    side = (1 - hi) * 2 + lo
    mate = hi * 2 + (1 - lo)
    cross = (1 - hi) * 2 + (1 - lo)
    rows, width = x_ref.shape
    n_keys = keys.shape[1]
    quarter = n_keys // nd
    new = kin_ref.shape[0]
    share = grad_ref.shape[0]

    loads = [
        pltpu.make_async_copy(src, dst, load_sem.at[i])
        for i, (src, dst) in enumerate(
            (
                (x_hbm, x_ref),
                (wq_hbm, wq_ref),
                (keys_hbm, keys.at[q]),
                (kin_hbm, kin_ref),
                (wk_hbm, wk_ref),
            )
        )
    ]
    for load in loads:
        load.start()

    def piece(r, part_of):
        return keys.at[r, pl.ds(pl.multiple_of(part_of * quarter, quarter), quarter)]

    def remote(src, dst, send, recv, where):
        return pltpu.make_async_remote_copy(
            src_ref=src, dst_ref=dst, send_sem=send, recv_sem=recv,
            device_id=where, device_id_type=MESH,
        )

    own_piece = keys_hbm.at[pl.ds(pl.multiple_of(d * quarter, quarter), quarter)]

    def key_up(r, src=None):
        src = piece(r, d) if src is None else src
        return remote(src, piece(r, d), up_send.at[r], z_recv.at[r], {"queue": jnp.minimum(q + 1, nq - 1)})

    def key_down(r, src=None):
        src = piece(r, d) if src is None else src
        return remote(src, piece(r, d), down_send.at[r], z_recv.at[r], {"queue": jnp.maximum(q - 1, 0)})

    def key_side(r):
        return remote(piece(r, d), piece(r, d), x_send.at[r], x_recv.at[r], {"dp": side})

    def key_side_in(r):
        return remote(piece(r, side), piece(r, side), x_send.at[r], x_recv.at[r], {"dp": side})

    def key_mate(r, k, part_of):
        return remote(piece(r, part_of), piece(r, part_of), c_send.at[r, k], c_recv.at[r, k], {"dp": mate})

    barrier = pltpu.get_barrier_semaphore()
    pl.semaphore_signal(barrier, inc=1, device_id={"dp": side}, device_id_type=MESH)
    pl.semaphore_signal(barrier, inc=1, device_id={"dp": mate}, device_id_type=MESH)
    for r in range(nq):
        @pl.when(q != r)
        def _():
            pl.semaphore_signal(barrier, inc=1, device_id={"queue": r}, device_id_type=MESH)
    pl.semaphore_wait(barrier, nq + 1)

    @pl.when(q < nq - 1)
    def _():
        key_up(q, own_piece).start()

    @pl.when(q > 0)
    def _():
        key_down(q, own_piece).start()

    loads[0].wait()
    loads[1].wait()
    query = jnp.dot(x_ref[...], wq_ref[...], preferred_element_type=F32)
    scale = lax.rsqrt(jnp.sum(query * query, -1, keepdims=True) + 1e-06)
    inv_len[...] = scale
    query = query * scale
    unit_f[...] = query
    unit[...] = query.astype(BF16)
    top[...] = jnp.full(top.shape, -1e30, F32)
    total[...] = jnp.zeros(total.shape, F32)
    posit[...] = jnp.zeros(posit.shape, F32)
    mixture[...] = jnp.zeros(mixture.shape, F32)
    chosen[...] = jnp.zeros(chosen.shape, F32)
    eye = lax.broadcasted_iota(jnp.int32, (rows, rows), 0) == lax.broadcasted_iota(
        jnp.int32, (rows, rows), 1
    )
    pos_col[...] = jnp.sum(jnp.where(eye, index_ref[...], 0), -1, keepdims=True)

    def fold(r):
        block = keys[r]
        scores = dot(unit[...], block, 1, 1) / temper
        hit = lax.broadcasted_iota(jnp.int32, (rows, n_keys), 1) + r * n_keys == pos_col[...]
        posit[...] += jnp.sum(jnp.where(hit, scores, 0.0), -1, keepdims=True)
        old = top[...]
        high = jnp.maximum(old, jnp.max(scores, -1, keepdims=True))
        decay = jnp.exp(old - high)
        expo = jnp.exp(scores - high)
        top[...] = high
        total[...] = total[...] * decay + jnp.sum(expo, -1, keepdims=True)
        mixture[...] = mixture[...] * decay + jnp.dot(
            expo.astype(BF16), block, preferred_element_type=F32
        )
        chosen[...] += jnp.dot(
            jnp.where(hit, 1.0, 0.0).astype(BF16), block, preferred_element_type=F32
        )

    loads[3].wait()
    loads[4].wait()
    made = jnp.dot(kin_ref[...], wk_ref[...], preferred_element_type=F32)
    made = (made * lax.rsqrt(jnp.sum(made * made, -1, keepdims=True) + 1e-06)).astype(BF16)
    fresh[d, pl.ds(pl.multiple_of(q * new, new), new)] = made

    def fresh_out(r):
        slot = fresh.at[d, pl.ds(pl.multiple_of(q * new, new), new)]
        return remote(slot, slot, fz_send.at[r], fz_recv.at[q], {"queue": r})

    def fresh_in(r):
        slot = fresh.at[d, pl.ds(pl.multiple_of(r * new, new), new)]
        return remote(slot, slot, fz_send.at[r], fz_recv.at[r], {"queue": r})

    def fresh_move(k, part_of, where):
        return remote(fresh.at[part_of], fresh.at[part_of], f_send.at[k], f_recv.at[k], {"dp": where})

    turned = x_ref[...].astype(F32).T
    for p in range(nd):
        xt[p] = jnp.concatenate(
            [turned[(r * nd + p) * share : (r * nd + p + 1) * share] for r in range(nq)], axis=0
        ).astype(BF16)

    loads[2].wait()
    fold(q)

    def others(s, act):
        @pl.when(q - s >= 0)
        def _():
            act(q - s, True)

        @pl.when(q + s <= nq - 1)
        def _():
            act(q + s, False)

    def pass_on(r, upward):
        key_side_in_z = remote(piece(r, d), piece(r, d), up_send.at[r], z_recv.at[r], {"dp": side})
        key_side_in_z.wait_recv()
        if upward:
            @pl.when(q < nq - 1)
            def _():
                key_up(r).start()
        else:
            @pl.when(q > 0)
            def _():
                key_down(r).start()
        key_side(r).start()
        key_mate(r, 0, d).start()

    def pass_side(r, upward):
        key_side_in(r).wait_recv()
        key_mate(r, 1, side).start()

    def take(r, upward):
        key_mate(r, 0, mate).wait_recv()
        key_mate(r, 1, cross).wait_recv()
        fold(r)

    def step(s, carry):
        @pl.when(s <= nq - 1)
        def _():
            others(s, pass_on)

        @pl.when(s == nq - 1)
        def _():
            for r in range(nq):
                @pl.when(q != r)
                def _():
                    fresh_out(r).start()

        @pl.when(s >= 2)
        def _():
            others(s - 1, pass_side)

            def both(k, carry):
                r = q + (s - 1) * (2 * k - 1)

                @pl.when((r >= 0) & (r <= nq - 1))
                def _():
                    take(r, True)

                return carry

            lax.fori_loop(0, 2, both, 0)

        return carry

    lax.fori_loop(1, nq + 1, step, 0)

    for r in range(nq):
        @pl.when(q != r)
        def _():
            fresh_in(r).wait_recv()
    fresh_move(0, d, side).start()
    fresh_move(1, d, mate).start()

    count = total[...]
    loss_col = top[...] + jnp.log(count) - posit[...]
    loss_ref[...] = jnp.sum(jnp.where(eye, loss_col, 0.0), 0, keepdims=True)
    grad_unit = (mixture[...] / count - chosen[...]) / temper
    units = unit_f[...]
    grad_q[...] = (
        (grad_unit - units * jnp.sum(units * grad_unit, -1, keepdims=True)) * inv_len[...]
    ).astype(BF16)

    def term(p):
        return jnp.dot(xt[p], grad_q[...], preferred_element_type=F32)

    def grad_mate(k):
        return remote(core_out.at[k], core_in.at[k], gc_send.at[k], gc_recv.at[k], {"dp": mate})

    def grad_side(r):
        return remote(x_out.at[r], x_in.at[r], gx_send.at[r], gx_recv.at[r], {"dp": side})

    def grad_up(r):
        return remote(z_out.at[r], up_in.at[r], gu_send.at[r], gu_recv.at[r], {"queue": jnp.minimum(q + 1, nq - 1)})

    def grad_down(r):
        return remote(z_out.at[r], down_in.at[r], gd_send.at[r], gd_recv.at[r], {"queue": jnp.maximum(q - 1, 0)})

    core_out[0] = term(cross).reshape(nq, share, width).astype(BF16)
    grad_mate(0).start()
    core_out[1] = term(mate).reshape(nq, share, width).astype(BF16)
    grad_mate(1).start()
    far = term(side).reshape(nq, share, width)
    part[...] = far
    grad_mate(0).wait_recv()
    x_out[...] = (part[...] + core_in[0].astype(F32)).astype(BF16)

    def in_turn(t, act_up, act_down):
        for_up = nq - 1 - (t - q)

        @pl.when((t >= q) & (for_up > q))
        def _():
            act_up(for_up)

        for_down = t - (nq - 1 - q)

        @pl.when((for_down >= 0) & (for_down < q))
        def _():
            act_down(for_down)

    def send_side(t, carry):
        in_turn(t, lambda r: grad_side(r).start(), lambda r: grad_side(r).start())
        return carry

    lax.fori_loop(0, nq - 1, send_side, 0)
    grad_side(q).start()

    part[...] = term(d).reshape(nq, share, width)
    fresh_move(0, side, side).wait_recv()
    fresh_move(2, side, mate).start()
    grad_mate(1).wait_recv()
    part[...] += core_in[1].astype(F32)

    fresh_move(1, mate, mate).wait_recv()
    fresh_move(2, cross, mate).wait_recv()
    n_new = nd * nq * new
    column = lax.broadcasted_iota(jnp.int32, (1, n_new), 1)
    block = (column % (nq * new)) // new * nd + column // (nq * new)
    goes = jnp.zeros((1, n_new), jnp.int32)
    for b in range(nd * nq):
        goes = jnp.where(block == b, owner_ref[b], goes)
    goes = goes * new + column % new - q * (nd * new)
    offset = lax.broadcasted_iota(jnp.int32, (n_keys, 1), 0) - pointer_ref[0]
    offset = jnp.where(offset < 0, offset + n_keys, offset)
    pick = jnp.where((goes == offset) & (offset < nd * new), 1.0, 0.0).astype(BF16)
    moved = jnp.dot(pick, fresh[...].reshape(n_new, width), preferred_element_type=F32)
    queue_ref[...] = jnp.where(offset < nd * new, moved, keys[q].astype(F32)).astype(BF16)

    def up_step(r):
        grad_side(r).wait_recv()
        part[r] += x_in[r].astype(F32)

        @pl.when(q > 0)
        def _():
            grad_up(r).wait_recv()
            part[r] += up_in[r].astype(F32)

        z_out[r] = part[r].astype(BF16)
        grad_up(r).start()

    def down_step(r):
        grad_side(r).wait_recv()
        part[r] += x_in[r].astype(F32)

        @pl.when(q < nq - 1)
        def _():
            grad_down(r).wait_recv()
            part[r] += down_in[r].astype(F32)

        z_out[r] = part[r].astype(BF16)
        grad_down(r).start()

    def chain(t, carry):
        in_turn(t, up_step, down_step)
        return carry

    lax.fori_loop(0, nq - 1, chain, 0)
    grad_side(q).wait_recv()
    part[q] += x_in[q].astype(F32)

    @pl.when(q > 0)
    def _():
        grad_up(q).wait_recv()
        part[q] += up_in[q].astype(F32)

    @pl.when(q < nq - 1)
    def _():
        grad_down(q).wait_recv()
        part[q] += down_in[q].astype(F32)

    grad_ref[...] = part[q]

    def drain(r, carry):
        @pl.when((r <= q) & (q < nq - 1))
        def _():
            key_up(r).wait_send()

        @pl.when((r >= q) & (q > 0))
        def _():
            key_down(r).wait_send()

        @pl.when(r != q)
        def _():
            key_side(r).wait_send()
            key_mate(r, 0, d).wait_send()
            key_mate(r, 1, side).wait_send()
            fresh_out(r).wait_send()

        grad_side(r).wait_send()

        @pl.when(r > q)
        def _():
            grad_up(r).wait_send()

        @pl.when(r < q)
        def _():
            grad_down(r).wait_send()

        return carry

    lax.fori_loop(0, nq, drain, 0)
    fresh_move(0, d, side).wait_send()
    fresh_move(1, d, mate).wait_send()
    fresh_move(2, side, mate).wait_send()
    grad_mate(0).wait_send()
    grad_mate(1).wait_send()


def make_body(nq, nd):

    def body(
        query_inputs, key_inputs, query_weight, key_weight,
        queue_keys, write_pointer, slot_owner, positive_index,
    ):
        rows, width = query_inputs.shape
        n_keys = queue_keys.shape[0]
        new = key_inputs.shape[0]
        share = width // (nq * nd)
        smem = pl.BlockSpec(memory_space=pltpu.SMEM)
        vmem = pl.BlockSpec(memory_space=pltpu.VMEM)
        hbm = pl.BlockSpec(memory_space=pl.ANY)
        V = pltpu.VMEM
        S = pltpu.SemaphoreType.DMA
        loss, grad, queue = pl.pallas_call(
            functools.partial(kernel, nq, nd),
            out_shape=(
                jax.ShapeDtypeStruct((1, rows), F32),
                jax.ShapeDtypeStruct((share, width), F32),
                jax.ShapeDtypeStruct((n_keys, width), BF16),
            ),
            in_specs=[smem, smem, vmem, hbm, hbm, hbm, hbm, hbm],
            out_specs=(vmem, vmem, vmem),
            scratch_shapes=[
                V((rows, width), BF16),
                V((new, width), BF16),
                V(query_weight.shape, BF16),
                V(key_weight.shape, BF16),
                V((nq, n_keys, width), BF16),
                V((nd, nq * new, width), BF16),
                V((rows, width), F32),
                V((rows, width), BF16),
                V((rows, 1), F32),
                V((rows, 1), F32),
                V((rows, 1), F32),
                V((rows, 1), F32),
                V((rows, 1), jnp.int32),
                V((rows, width), F32),
                V((rows, width), F32),
                V((nd, nq * share, rows), BF16),
                V((rows, width), BF16),
                V((2, nq, share, width), BF16),
                V((2, nq, share, width), BF16),
                V((nq, share, width), F32),
                V((nq, share, width), BF16),
                V((nq, share, width), BF16),
                V((nq, share, width), BF16),
                V((nq, share, width), BF16),
                V((nq, share, width), BF16),
                S((5,)), S((nq,)), S((nq,)), S((nq,)), S((nq,)), S((nq,)), S((nq, 2)), S((nq, 2)),
                S((nq,)), S((nq,)), S((3,)), S((3,)),
                S((2,)), S((2,)), S((nq,)), S((nq,)), S((nq,)), S((nq,)), S((nq,)), S((nq,)),
            ],
            compiler_params=pltpu.CompilerParams(
                collective_id=0, has_side_effects=True, vmem_limit_bytes=56 * 2**20
            ),
            name="contrast",
        )(
            write_pointer, slot_owner, positive_index.reshape(1, rows),
            query_inputs, key_inputs, query_weight, key_weight, queue_keys,
        )
        return loss.reshape(rows), grad, queue

    return body


def solution(mesh):
    in_specs = (
        P(("groups", "queue", "dp"), None),
        P(("groups", "queue", "dp"), None),
        P(),
        P(),
        P(("groups", "queue"), None),
        P("groups"),
        P("groups"),
        P(("groups", "queue", "dp")),
    )
    out_specs = (
        P(("groups", "queue", "dp")),
        P(("groups", "queue", "dp"), None),
        P(("groups", "queue"), None),
    )
    body = make_body(mesh.shape["queue"], mesh.shape["dp"])
    return jax.shard_map(body, mesh=mesh, in_specs=in_specs, out_specs=out_specs, check_vma=False)
```

```python
import functools

import jax
import jax.numpy as jnp
from jax import lax
from jax.experimental import pallas as pl
from jax.experimental.pallas import tpu as pltpu
from jax.sharding import PartitionSpec as P

temper = 0.05
splits = 2
cuts = 4
MESH = pl.DeviceIdType.MESH
F32 = jnp.float32
BF16 = jnp.bfloat16


def dot(a, b, da, db):
    return lax.dot_general(a, b, (((da,), (db,)), ((), ())), preferred_element_type=F32)


def kernel(
    nq, nd,
    pointer_hbm, owner_hbm, index_hbm, x_hbm, kin_hbm, wq_hbm, wk_hbm, keys_hbm,
    loss_hbm, grad_hbm, queue_hbm,
    pointer_ref, owner_ref, index_ref, loss_ref, queue_ref,
    x_ref, kin_ref, wq_ref, wk_ref, keys, fresh,
    unit_f, unit, inv_len, top, total, posit, pos_col, mixture, chosen,
    xt, grad_q, core_out, core_in, keep_out, keep_in, part, x_out, x_in, up_in, down_in, z_out,
    load_sem, store_sem, up_send, down_send, z_recv, x_send, x_recv, c_send, c_recv,
    fz_send, fz_recv, f_send, f_recv,
    gc_send, gc_recv, gk_send, gk_recv, gx_send, gx_recv, gu_send, gd_send, gu_recv, gd_recv,
):
    q = lax.axis_index("queue")
    d = lax.axis_index("dp")
    hi, lo = d // 2, d % 2
    side = (1 - hi) * 2 + lo
    mate = hi * 2 + (1 - lo)
    cross = (1 - hi) * 2 + (1 - lo)
    rows, width = x_ref.shape
    n_keys = keys.shape[1]
    quarter = n_keys // nd
    new = kin_ref.shape[0]
    blocks = part.shape[0]
    sub = blocks // nq
    share = grad_hbm.shape[0]
    thin = share // sub
    cut = quarter // sub
    micro = (nq - 1) * sub

    loads = [
        pltpu.make_async_copy(src, dst, load_sem.at[i])
        for i, (src, dst) in enumerate(
            (
                (x_hbm, x_ref),
                (wq_hbm, wq_ref),
                (keys_hbm, keys.at[q]),
                (kin_hbm, kin_ref),
                (wk_hbm, wk_ref),
                (index_hbm, index_ref),
                (owner_hbm, owner_ref),
                (pointer_hbm, pointer_ref),
            )
        )
    ]
    for load in loads:
        load.start()

    def piece(k, part_of):
        start = part_of * quarter + lax.rem(k, sub) * cut
        return keys.at[k // sub, pl.ds(pl.multiple_of(start, cut), cut)]

    def remote(src, dst, send, recv, where):
        return pltpu.make_async_remote_copy(
            src_ref=src, dst_ref=dst, send_sem=send, recv_sem=recv,
            device_id=where, device_id_type=MESH,
        )

    above = {"queue": jnp.minimum(q + 1, nq - 1)}
    below = {"queue": jnp.maximum(q - 1, 0)}

    def own_piece(h):
        return keys_hbm.at[pl.ds(pl.multiple_of(d * quarter + h * cut, cut), cut)]

    def key_up(k, src=None):
        src = piece(k, d) if src is None else src
        return remote(src, piece(k, d), up_send.at[k], z_recv.at[k], above)

    def key_down(k, src=None):
        src = piece(k, d) if src is None else src
        return remote(src, piece(k, d), down_send.at[k], z_recv.at[k], below)

    def key_side(k):
        return remote(piece(k, d), piece(k, d), x_send.at[k], x_recv.at[k], {"dp": side})

    def key_side_in(k):
        return remote(piece(k, side), piece(k, side), x_send.at[k], x_recv.at[k], {"dp": side})

    def key_mate(k, i, part_of):
        return remote(piece(k, part_of), piece(k, part_of), c_send.at[k, i], c_recv.at[k, i], {"dp": mate})

    barrier = pltpu.get_barrier_semaphore()
    pl.semaphore_signal(barrier, inc=1, device_id={"dp": side}, device_id_type=MESH)
    pl.semaphore_signal(barrier, inc=1, device_id={"dp": mate}, device_id_type=MESH)
    for r in range(nq):
        @pl.when(q != r)
        def _():
            pl.semaphore_signal(barrier, inc=1, device_id={"queue": r}, device_id_type=MESH)
    pl.semaphore_wait(barrier, nq + 1)

    for h in range(sub):
        @pl.when(q < nq - 1)
        def _():
            key_up(q * sub + h, own_piece(h)).start()

        @pl.when(q > 0)
        def _():
            key_down(q * sub + h, own_piece(h)).start()

    loads[0].wait()
    loads[1].wait()
    query = jnp.dot(x_ref[...], wq_ref[...], preferred_element_type=F32)
    scale = lax.rsqrt(jnp.sum(query * query, -1, keepdims=True) + 1e-06)
    inv_len[...] = scale
    query = query * scale
    unit_f[...] = query
    unit[...] = query.astype(BF16)
    top[...] = jnp.full(top.shape, -1e30, F32)
    total[...] = jnp.zeros(total.shape, F32)
    posit[...] = jnp.zeros(posit.shape, F32)
    mixture[...] = jnp.zeros(mixture.shape, F32)
    chosen[...] = jnp.zeros(chosen.shape, F32)
    eye = lax.broadcasted_iota(jnp.int32, (rows, rows), 0) == lax.broadcasted_iota(
        jnp.int32, (rows, rows), 1
    )
    loads[5].wait()
    pos_col[...] = jnp.sum(jnp.where(eye, index_ref[...], 0), -1, keepdims=True)

    def fold(r):
        block = keys[r]
        scores = dot(unit[...], block, 1, 1) / temper
        hit = lax.broadcasted_iota(jnp.int32, (rows, n_keys), 1) + r * n_keys == pos_col[...]
        posit[...] += jnp.sum(jnp.where(hit, scores, 0.0), -1, keepdims=True)
        old = top[...]
        high = jnp.maximum(old, jnp.max(scores, -1, keepdims=True))
        decay = jnp.exp(old - high)
        expo = jnp.exp(scores - high)
        top[...] = high
        total[...] = total[...] * decay + jnp.sum(expo, -1, keepdims=True)
        mixture[...] = mixture[...] * decay + jnp.dot(
            expo.astype(BF16), block, preferred_element_type=F32
        )
        chosen[...] += jnp.dot(
            jnp.where(hit, 1.0, 0.0).astype(BF16), block, preferred_element_type=F32
        )

    def make_fresh():
        loads[3].wait()
        loads[4].wait()
        made = jnp.dot(kin_ref[...], wk_ref[...], preferred_element_type=F32)
        made = (made * lax.rsqrt(jnp.sum(made * made, -1, keepdims=True) + 1e-06)).astype(BF16)
        fresh[d, pl.ds(pl.multiple_of(q * new, new), new)] = made

    def fresh_out(r):
        slot = fresh.at[d, pl.ds(pl.multiple_of(q * new, new), new)]
        return remote(slot, slot, fz_send.at[r], fz_recv.at[q], {"queue": r})

    def fresh_in(r):
        slot = fresh.at[d, pl.ds(pl.multiple_of(r * new, new), new)]
        return remote(slot, slot, fz_send.at[r], fz_recv.at[r], {"queue": r})

    def fresh_move(k, part_of, where):
        return remote(fresh.at[part_of], fresh.at[part_of], f_send.at[k], f_recv.at[k], {"dp": where})

    def turn():
        turned = x_ref[...].astype(F32).T
        for p in range(nd):
            xt[p] = jnp.concatenate(
                [turned[(r * nd + p) * share : (r * nd + p + 1) * share] for r in range(nq)], axis=0
            ).astype(BF16)

    loads[2].wait()
    fold(q)

    def others(m, act):
        s, h = m // sub + 1, lax.rem(m, sub)

        @pl.when(q - s >= 0)
        def _():
            act((q - s) * sub + h, True)

        @pl.when(q + s <= nq - 1)
        def _():
            act((q + s) * sub + h, False)

    def pass_on(k, upward):
        key_up(k).wait_recv()
        if upward:
            @pl.when(q < nq - 1)
            def _():
                key_up(k).start()
        else:
            @pl.when(q > 0)
            def _():
                key_down(k).start()
        key_side(k).start()
        key_mate(k, 0, d).start()

    def pass_side(k, upward):
        key_side_in(k).wait_recv()
        key_mate(k, 1, side).start()

    def step(m, carry):
        @pl.when(m < micro)
        def _():
            others(m, pass_on)

        @pl.when(m == 0)
        def _():
            make_fresh()

        @pl.when(m == 1)
        def _():
            turn()

        @pl.when(m == micro - 1)
        def _():
            for r in range(nq):
                @pl.when(q != r)
                def _():
                    fresh_out(r).start()

        @pl.when((m >= 2) & (m < micro + 2))
        def _():
            others(m - 2, pass_side)

        @pl.when((m >= 3) & (lax.rem(m, sub) == (sub + 2) % sub))
        def _():
            def both(i, carry):
                r = q + ((m - 3) // sub + 1) * (2 * i - 1)

                @pl.when((r >= 0) & (r <= nq - 1))
                def _():
                    for h in range(sub):
                        key_mate(r * sub + h, 0, mate).wait_recv()
                        key_mate(r * sub + h, 1, cross).wait_recv()
                    fold(r)

                return carry

            lax.fori_loop(0, 2, both, 0)

        return carry

    lax.fori_loop(0, micro + 3, step, 0)

    for r in range(nq):
        @pl.when(q != r)
        def _():
            fresh_in(r).wait_recv()
    fresh_move(0, d, side).start()
    fresh_move(1, d, mate).start()

    count = total[...]
    grad_unit = mixture[...] * (1.0 / (count * temper)) - chosen[...] * (1.0 / temper)
    units = unit_f[...]
    grad_q[...] = (
        (grad_unit - units * jnp.sum(units * grad_unit, -1, keepdims=True)) * inv_len[...]
    ).astype(BF16)

    def term(p):
        return jnp.dot(xt[p], grad_q[...], preferred_element_type=F32).reshape(blocks, thin, width)

    def grad_mate(k):
        return remote(core_out.at[k], core_in.at[k], gc_send.at[k], gc_recv.at[k], {"dp": mate})

    def grad_keep():
        return remote(keep_out, keep_in, gk_send.at[0], gk_recv.at[0], {"dp": mate})

    def grad_side(k):
        return remote(x_out.at[k], x_in.at[k], gx_send.at[k], gx_recv.at[k], {"dp": side})

    def grad_up(k):
        return remote(z_out.at[k], up_in.at[k], gu_send.at[k], gu_recv.at[k], above)

    def grad_down(k):
        return remote(z_out.at[k], down_in.at[k], gd_send.at[k], gd_recv.at[k], below)

    def in_turn(act_up, act_down, act_own):
        def at(t, carry):
            for_up = nq - 1 - (t - q)
            for_down = t - (nq - 1 - q)
            for h in range(sub):
                @pl.when((t >= q) & (for_up > q))
                def _():
                    act_up(for_up * sub + h)

                @pl.when((for_down >= 0) & (for_down < q))
                def _():
                    act_down(for_down * sub + h)

            return carry

        lax.fori_loop(0, nq - 1, at, 0)
        for h in range(sub):
            act_own(q * sub + h)

    def start_mate(k):
        grad_mate(k).start()

    core_out[...] = term(cross).astype(BF16)
    in_turn(start_mate, start_mate, start_mate)
    part[...] = term(side)
    keep_out[...] = term(mate).astype(BF16)
    grad_keep().start()

    def start_side(k):
        grad_mate(k).wait_recv()
        x_out[k] = (part[k] + core_in[k].astype(F32)).astype(BF16)
        grad_side(k).start()

    in_turn(start_side, start_side, start_side)
    fresh_move(0, side, side).wait_recv()
    fresh_move(2, side, mate).start()
    part[...] = term(d)
    grad_keep().wait_recv()
    part[...] += keep_in[...].astype(F32)

    loss_col = top[...] + jnp.log(count) - posit[...]
    loss_ref[...] = jnp.sum(jnp.where(eye, loss_col, 0.0), 0, keepdims=True)
    stores = [
        pltpu.make_async_copy(loss_ref, loss_hbm, store_sem.at[0]),
        pltpu.make_async_copy(queue_ref, queue_hbm, store_sem.at[1]),
    ]
    stores[0].start()

    loads[6].wait()
    loads[7].wait()
    fresh_move(1, mate, mate).wait_recv()
    fresh_move(2, cross, mate).wait_recv()
    n_new = nd * nq * new
    column = lax.broadcasted_iota(jnp.int32, (1, n_new), 1)
    block = (column % (nq * new)) // new * nd + column // (nq * new)
    goes = jnp.zeros((1, n_new), jnp.int32)
    for b in range(nd * nq):
        goes = jnp.where(block == b, owner_ref[b], goes)
    goes = goes * new + column % new - q * (nd * new)
    offset = lax.broadcasted_iota(jnp.int32, (n_keys, 1), 0) - pointer_ref[0]
    offset = jnp.where(offset < 0, offset + n_keys, offset)
    pick = jnp.where((goes == offset) & (offset < nd * new), 1.0, 0.0).astype(BF16)
    moved = jnp.dot(pick, fresh[...].reshape(n_new, width), preferred_element_type=F32)
    queue_ref[...] = jnp.where(offset < nd * new, moved, keys[q].astype(F32)).astype(BF16)

    stores[1].start()

    def up_step(k):
        grad_side(k).wait_recv()
        part[k] += x_in[k].astype(F32)

        @pl.when(q > 0)
        def _():
            grad_up(k).wait_recv()
            part[k] += up_in[k].astype(F32)

        z_out[k] = part[k].astype(BF16)
        grad_up(k).start()

    def down_step(k):
        grad_side(k).wait_recv()
        part[k] += x_in[k].astype(F32)

        @pl.when(q < nq - 1)
        def _():
            grad_down(k).wait_recv()
            part[k] += down_in[k].astype(F32)

        z_out[k] = part[k].astype(BF16)
        grad_down(k).start()

    def own_out(h):
        return pltpu.make_async_copy(
            part.at[q * sub + h], grad_hbm.at[pl.ds(h * thin, thin)], store_sem.at[2 + h]
        )

    def own_step(k):
        grad_side(k).wait_recv()
        part[k] += x_in[k].astype(F32)

        @pl.when(q > 0)
        def _():
            grad_up(k).wait_recv()
            part[k] += up_in[k].astype(F32)

        @pl.when(q < nq - 1)
        def _():
            grad_down(k).wait_recv()
            part[k] += down_in[k].astype(F32)

    in_turn(up_step, down_step, lambda k: None)
    for h in range(sub):
        own_step(q * sub + h)
        own_out(h).start()

    def drain(k, carry):
        r = k // sub

        @pl.when((r <= q) & (q < nq - 1))
        def _():
            key_up(k).wait_send()

        @pl.when((r >= q) & (q > 0))
        def _():
            key_down(k).wait_send()

        @pl.when(r != q)
        def _():
            key_side(k).wait_send()
            key_mate(k, 0, d).wait_send()
            key_mate(k, 1, side).wait_send()

        grad_mate(k).wait_send()
        grad_side(k).wait_send()

        @pl.when(r > q)
        def _():
            grad_up(k).wait_send()

        @pl.when(r < q)
        def _():
            grad_down(k).wait_send()

        return carry

    lax.fori_loop(0, blocks, drain, 0)
    for r in range(nq):
        @pl.when(q != r)
        def _():
            fresh_out(r).wait_send()
    fresh_move(0, d, side).wait_send()
    fresh_move(1, d, mate).wait_send()
    fresh_move(2, side, mate).wait_send()
    grad_keep().wait_send()
    for store in stores:
        store.wait()
    for h in range(sub):
        own_out(h).wait()


def finish(cuts, loss_in, grad_in, queue_in, loss_out, grad_out, queue_out, sem):
    copies = [pltpu.make_async_copy(loss_in, loss_out, sem.at[0])]
    for src, dst in ((grad_in, grad_out), (queue_in, queue_out)):
        n = src.shape[0] // cuts if src.shape[0] % (16 * cuts) == 0 else src.shape[0]
        for at in range(0, src.shape[0], n):
            piece = pl.ds(at, n)
            copies.append(pltpu.make_async_copy(src.at[piece], dst.at[piece], sem.at[len(copies)]))
    for copy in copies:
        copy.start()
    for copy in copies:
        copy.wait()


def make_body(nq, nd):

    def body(
        query_inputs, key_inputs, query_weight, key_weight,
        queue_keys, write_pointer, slot_owner, positive_index,
    ):
        rows, width = query_inputs.shape
        n_keys = queue_keys.shape[0]
        new = key_inputs.shape[0]
        share = width // (nq * nd)
        sub = splits if share % (16 * splits) == 0 else 1
        blocks, thin = nq * sub, share // sub
        hbm = pl.BlockSpec(memory_space=pl.ANY)
        V = pltpu.VMEM
        S = pltpu.SemaphoreType.DMA
        outs = (
            jax.ShapeDtypeStruct((1, rows), F32),
            jax.ShapeDtypeStruct((share, width), F32),
            jax.ShapeDtypeStruct((n_keys, width), BF16),
        )
        each = S((blocks,))
        made = pl.pallas_call(
            functools.partial(kernel, nq, nd),
            out_shape=outs,
            in_specs=[hbm] * 8,
            out_specs=(hbm,) * 3,
            scratch_shapes=[
                pltpu.SMEM(write_pointer.shape, jnp.int32),
                pltpu.SMEM(slot_owner.shape, jnp.int32),
                V((1, rows), jnp.int32),
                V((1, rows), F32),
                V((n_keys, width), BF16),
                V((rows, width), BF16),
                V((new, width), BF16),
                V(query_weight.shape, BF16),
                V(key_weight.shape, BF16),
                V((nq, n_keys, width), BF16),
                V((nd, nq * new, width), BF16),
                V((rows, width), F32),
                V((rows, width), BF16),
                V((rows, 1), F32),
                V((rows, 1), F32),
                V((rows, 1), F32),
                V((rows, 1), F32),
                V((rows, 1), jnp.int32),
                V((rows, width), F32),
                V((rows, width), F32),
                V((nd, nq * share, rows), BF16),
                V((rows, width), BF16),
                V((blocks, thin, width), BF16),
                V((blocks, thin, width), BF16),
                V((blocks, thin, width), BF16),
                V((blocks, thin, width), BF16),
                V((blocks, thin, width), F32),
                V((blocks, thin, width), BF16),
                V((blocks, thin, width), BF16),
                V((blocks, thin, width), BF16),
                V((blocks, thin, width), BF16),
                V((blocks, thin, width), BF16),
                S((8,)), S((2 + sub,)), each, each, each, each, each, S((blocks, 2)), S((blocks, 2)),
                S((nq,)), S((nq,)), S((3,)), S((3,)),
                each, each, S((1,)), S((1,)), each, each, each, each, each, each,
            ],
            compiler_params=pltpu.CompilerParams(
                collective_id=0, has_side_effects=True, vmem_limit_bytes=56 * 2**20
            ),
            name="contrast",
        )(
            write_pointer, slot_owner, positive_index.reshape(1, rows),
            query_inputs, key_inputs, query_weight, key_weight, queue_keys,
        )
        loss, grad, queue = pl.pallas_call(
            functools.partial(finish, cuts),
            out_shape=outs,
            in_specs=[hbm] * 3,
            out_specs=(hbm,) * 3,
            scratch_shapes=[S((1 + 2 * cuts,))],
            name="finish",
        )(*made)
        return loss.reshape(rows), grad, queue

    return body


def solution(mesh):
    in_specs = (
        P(("groups", "queue", "dp"), None),
        P(("groups", "queue", "dp"), None),
        P(),
        P(),
        P(("groups", "queue"), None),
        P("groups"),
        P("groups"),
        P(("groups", "queue", "dp")),
    )
    out_specs = (
        P(("groups", "queue", "dp")),
        P(("groups", "queue", "dp"), None),
        P(("groups", "queue"), None),
    )
    body = make_body(mesh.shape["queue"], mesh.shape["dp"])
    return jax.shard_map(body, mesh=mesh, in_specs=in_specs, out_specs=out_specs, check_vma=False)
```

```python
import functools

import jax
import jax.numpy as jnp
from jax import lax
from jax.experimental import pallas as pl
from jax.experimental.pallas import tpu as pltpu
from jax.sharding import PartitionSpec as P

temper = 0.05
splits = 2
tile = 256
strip = 32
MESH = pl.DeviceIdType.MESH
F32 = jnp.float32
BF16 = jnp.bfloat16


def dot(a, b, da, db):
    return lax.dot_general(a, b, (((da,), (db,)), ((), ())), preferred_element_type=F32)


def kernel(
    nq, nd,
    pointer_hbm, owner_hbm, index_hbm, x_hbm, kin_hbm, wq_hbm, wk_hbm, keys_hbm,
    loss_hbm, grad_hbm, queue_hbm,
    pointer_ref, owner_ref, index_ref, loss_ref, queue_ref, pair, fade, made_f, picks,
    x_ref, kin_ref, wq_ref, wk_ref, keys, fresh,
    unit_f, unit, inv_len, top, total, posit, pos_col, mixture, chosen,
    xt, grad_q, core_out, core_in, keep_out, keep_in, part, x_out, x_in, up_in, down_in, z_out,
    load_sem, store_sem, up_send, down_send, z_recv, x_send, x_recv, c_send, c_recv,
    fz_send, fz_recv, f_send, f_recv,
    gc_send, gc_recv, gk_send, gk_recv, gx_send, gx_recv, gu_send, gd_send, gu_recv, gd_recv,
):
    q = lax.axis_index("queue")
    d = lax.axis_index("dp")
    hi, lo = d // 2, d % 2
    side = (1 - hi) * 2 + lo
    mate = hi * 2 + (1 - lo)
    cross = (1 - hi) * 2 + (1 - lo)
    rows, width = x_ref.shape
    n_keys = keys.shape[1]
    quarter = n_keys // nd
    new = kin_ref.shape[0]
    blocks = part.shape[0]
    sub = blocks // nq
    share = grad_hbm.shape[0]
    thin = share // sub
    cut = quarter // sub
    micro = (nq - 1) * sub

    loads = [
        pltpu.make_async_copy(src, dst, load_sem.at[i])
        for i, (src, dst) in enumerate(
            (
                (x_hbm, x_ref),
                (wq_hbm, wq_ref),
                (keys_hbm, keys.at[q]),
                (kin_hbm, kin_ref),
                (wk_hbm, wk_ref),
                (index_hbm, index_ref),
                (owner_hbm, owner_ref),
                (pointer_hbm, pointer_ref),
            )
        )
    ]
    for load in loads:
        load.start()

    def piece(k, part_of):
        start = part_of * quarter + lax.rem(k, sub) * cut
        return keys.at[k // sub, pl.ds(pl.multiple_of(start, cut), cut)]

    def remote(src, dst, send, recv, where):
        return pltpu.make_async_remote_copy(
            src_ref=src, dst_ref=dst, send_sem=send, recv_sem=recv,
            device_id=where, device_id_type=MESH,
        )

    above = {"queue": jnp.minimum(q + 1, nq - 1)}
    below = {"queue": jnp.maximum(q - 1, 0)}

    def own_piece(h):
        return keys_hbm.at[pl.ds(pl.multiple_of(d * quarter + h * cut, cut), cut)]

    def key_up(k, src=None):
        src = piece(k, d) if src is None else src
        return remote(src, piece(k, d), up_send.at[k], z_recv.at[k], above)

    def key_down(k, src=None):
        src = piece(k, d) if src is None else src
        return remote(src, piece(k, d), down_send.at[k], z_recv.at[k], below)

    def key_side(k):
        return remote(piece(k, d), piece(k, d), x_send.at[k], x_recv.at[k], {"dp": side})

    def key_side_in(k):
        return remote(piece(k, side), piece(k, side), x_send.at[k], x_recv.at[k], {"dp": side})

    def key_mate(k, i, part_of):
        return remote(piece(k, part_of), piece(k, part_of), c_send.at[k, i], c_recv.at[k, i], {"dp": mate})

    barrier = pltpu.get_barrier_semaphore()
    pl.semaphore_signal(barrier, inc=1, device_id={"dp": side}, device_id_type=MESH)
    pl.semaphore_signal(barrier, inc=1, device_id={"dp": mate}, device_id_type=MESH)
    for r in range(nq):
        @pl.when(q != r)
        def _():
            pl.semaphore_signal(barrier, inc=1, device_id={"queue": r}, device_id_type=MESH)
    pl.semaphore_wait(barrier, nq + 1)

    for h in range(sub):
        @pl.when(q < nq - 1)
        def _():
            key_up(q * sub + h, own_piece(h)).start()

        @pl.when(q > 0)
        def _():
            key_down(q * sub + h, own_piece(h)).start()

    loads[0].wait()
    loads[1].wait()
    inv_len[...] = jnp.zeros(inv_len.shape, F32)

    @pl.loop(0, width // tile)
    def _(j):
        cols = pl.ds(pl.multiple_of(j * tile, tile), tile)
        query = jnp.dot(x_ref[...], wq_ref[:, cols], preferred_element_type=F32)
        unit_f[:, cols] = query
        inv_len[...] += jnp.sum(query * query, -1, keepdims=True)

    inv_len[...] = lax.rsqrt(inv_len[...] + 1e-06)

    @pl.loop(0, rows // strip)
    def _(i):
        at = pl.ds(pl.multiple_of(i * strip, strip), strip)
        query = unit_f[at] * inv_len[at]
        unit_f[at] = query
        unit[at] = query.astype(BF16)
        mixture[at] = jnp.zeros((strip, width), F32)
        chosen[at] = jnp.zeros((strip, width), F32)

    top[...] = jnp.full(top.shape, -1e30, F32)
    total[...] = jnp.zeros(total.shape, F32)
    posit[...] = jnp.zeros(posit.shape, F32)
    eye = lax.broadcasted_iota(jnp.int32, (rows, rows), 0) == lax.broadcasted_iota(
        jnp.int32, (rows, rows), 1
    )
    loads[5].wait()
    pos_col[...] = jnp.sum(jnp.where(eye, index_ref[...], 0), -1, keepdims=True)

    def fold(r):
        block = keys[r]
        scores = dot(unit[...], block, 1, 1) / temper
        hit = lax.broadcasted_iota(jnp.int32, (rows, n_keys), 1) + r * n_keys == pos_col[...]
        posit[...] += jnp.sum(jnp.where(hit, scores, 0.0), -1, keepdims=True)
        old = top[...]
        high = jnp.maximum(old, jnp.max(scores, -1, keepdims=True))
        decay = jnp.exp(old - high)
        expo = jnp.exp(scores - high)
        top[...] = high
        total[...] = total[...] * decay + jnp.sum(expo, -1, keepdims=True)
        pair[:rows] = expo.astype(BF16)
        pair[rows:] = jnp.where(hit, 1.0, 0.0).astype(BF16)
        fade[...] = decay

        @pl.loop(0, width // tile)
        def _(j):
            cols = pl.ds(pl.multiple_of(j * tile, tile), tile)
            both = jnp.dot(pair[...], keys[r, :, cols], preferred_element_type=F32)
            mixture[:, cols] = mixture[:, cols] * fade[...] + both[:rows]
            chosen[:, cols] += both[rows:]


    def make_fresh():
        loads[3].wait()
        loads[4].wait()

        @pl.loop(0, width // tile)
        def _(j):
            cols = pl.ds(pl.multiple_of(j * tile, tile), tile)
            made_f[:, cols] = jnp.dot(kin_ref[...], wk_ref[:, cols], preferred_element_type=F32)

        made = made_f[...]
        made = (made * lax.rsqrt(jnp.sum(made * made, -1, keepdims=True) + 1e-06)).astype(BF16)
        fresh[d, pl.ds(pl.multiple_of(q * new, new), new)] = made

    def fresh_out(r):
        slot = fresh.at[d, pl.ds(pl.multiple_of(q * new, new), new)]
        return remote(slot, slot, fz_send.at[r], fz_recv.at[q], {"queue": r})

    def fresh_in(r):
        slot = fresh.at[d, pl.ds(pl.multiple_of(r * new, new), new)]
        return remote(slot, slot, fz_send.at[r], fz_recv.at[r], {"queue": r})

    def fresh_move(k, part_of, where):
        return remote(fresh.at[part_of], fresh.at[part_of], f_send.at[k], f_recv.at[k], {"dp": where})

    def turn():
        if nd * share % 128 == 0:
            @pl.loop(0, nq)
            def _(r):
                cols = pl.ds(pl.multiple_of(r * nd * share, nd * share), nd * share)
                turned = x_ref[:, cols].astype(F32).T.astype(BF16)
                for p in range(nd):
                    xt[p, pl.ds(pl.multiple_of(r * share, share), share)] = turned[p * share : (p + 1) * share]

            return
        turned = x_ref[...].astype(F32).T
        for p in range(nd):
            xt[p] = jnp.concatenate(
                [turned[(r * nd + p) * share : (r * nd + p + 1) * share] for r in range(nq)], axis=0
            ).astype(BF16)

    def others(m, act):
        s, h = m // sub + 1, lax.rem(m, sub)

        @pl.when(q - s >= 0)
        def _():
            act((q - s) * sub + h, True)

        @pl.when(q + s <= nq - 1)
        def _():
            act((q + s) * sub + h, False)

    def pass_on(k, upward):
        key_up(k).wait_recv()
        if upward:
            @pl.when(q < nq - 1)
            def _():
                key_up(k).start()
        else:
            @pl.when(q > 0)
            def _():
                key_down(k).start()
        key_side(k).start()
        key_mate(k, 0, d).start()

    def pass_side(k, upward):
        key_side_in(k).wait_recv()
        key_mate(k, 1, side).start()

    def step(m, carry):
        @pl.when(m < micro)
        def _():
            others(m, pass_on)

        @pl.when(m == 0)
        def _():
            make_fresh()

        @pl.when(m == 1)
        def _():
            turn()

        @pl.when(m == micro - 1)
        def _():
            for r in range(nq):
                @pl.when(q != r)
                def _():
                    fresh_out(r).start()

        @pl.when((m >= 2) & (m < micro + 2))
        def _():
            others(m - 2, pass_side)

        @pl.when(m == 0)
        def _():
            loads[2].wait()

        def both(i, carry):
            r = jnp.where(m == 0, q, q + ((m - 3) // sub + 1) * (2 * i - 1))
            own = (m == 0) & (i == 0)
            later = (m >= 3) & (lax.rem(m, sub) == 2 % sub) & (r >= 0) & (r <= nq - 1)

            @pl.when(later)
            def _():
                for h in range(sub):
                    key_mate(r * sub + h, 0, mate).wait_recv()
                    key_mate(r * sub + h, 1, cross).wait_recv()

            @pl.when(own | later)
            def _():
                fold(r)

            return carry

        lax.fori_loop(0, 2, both, 0)

        return carry

    lax.fori_loop(0, micro + 3, step, 0)

    for r in range(nq):
        @pl.when(q != r)
        def _():
            fresh_in(r).wait_recv()
    fresh_move(0, d, side).start()
    fresh_move(1, d, mate).start()

    @pl.loop(0, rows // strip)
    def _(i):
        at = pl.ds(pl.multiple_of(i * strip, strip), strip)
        grad_unit = mixture[at] * (1.0 / (total[at] * temper)) - chosen[at] * (1.0 / temper)
        units = unit_f[at]
        grad_q[at] = (
            (grad_unit - units * jnp.sum(units * grad_unit, -1, keepdims=True)) * inv_len[at]
        ).astype(BF16)

    def term(p, out):
        @pl.loop(0, width // tile)
        def _(j):
            cols = pl.ds(pl.multiple_of(j * tile, tile), tile)
            got = jnp.dot(xt[p], grad_q[:, cols], preferred_element_type=F32)
            out[:, :, cols] = got.reshape(blocks, thin, tile).astype(out.dtype)

    def grad_mate(k):
        return remote(core_out.at[k], core_in.at[k], gc_send.at[k], gc_recv.at[k], {"dp": mate})

    def grad_keep():
        return remote(keep_out, keep_in, gk_send.at[0], gk_recv.at[0], {"dp": mate})

    def grad_side(k):
        return remote(x_out.at[k], x_in.at[k], gx_send.at[k], gx_recv.at[k], {"dp": side})

    def grad_up(k):
        return remote(z_out.at[k], up_in.at[k], gu_send.at[k], gu_recv.at[k], above)

    def grad_down(k):
        return remote(z_out.at[k], down_in.at[k], gd_send.at[k], gd_recv.at[k], below)

    def in_turn(act_up, act_down, act_own):
        def at(t, carry):
            for_up = nq - 1 - (t - q)
            for_down = t - (nq - 1 - q)

            def half(h, carry):
                @pl.when((t >= q) & (for_up > q))
                def _():
                    act_up(for_up * sub + h)

                @pl.when((for_down >= 0) & (for_down < q))
                def _():
                    act_down(for_down * sub + h)

                return carry

            lax.fori_loop(0, sub, half, 0)
            return carry

        lax.fori_loop(0, nq - 1, at, 0)
        for h in range(sub):
            act_own(q * sub + h)

    def start_mate(k):
        grad_mate(k).start()

    term(cross, core_out)
    in_turn(start_mate, start_mate, start_mate)
    term(side, part)
    term(mate, keep_out)
    grad_keep().start()

    def start_side(k):
        grad_mate(k).wait_recv()
        x_out[k] = (part[k] + core_in[k].astype(F32)).astype(BF16)
        grad_side(k).start()

    in_turn(start_side, start_side, start_side)
    fresh_move(0, side, side).wait_recv()
    fresh_move(2, side, mate).start()
    term(d, part)
    grad_keep().wait_recv()

    @pl.loop(0, blocks)
    def _(k):
        part[k] += keep_in[k].astype(F32)

    loss_col = top[...] + jnp.log(total[...]) - posit[...]
    loss_ref[...] = jnp.sum(jnp.where(eye, loss_col, 0.0), 0, keepdims=True)
    stores = [
        pltpu.make_async_copy(loss_ref, loss_hbm, store_sem.at[0]),
        pltpu.make_async_copy(queue_ref, queue_hbm, store_sem.at[1]),
    ]
    stores[0].start()

    loads[6].wait()
    loads[7].wait()
    fresh_move(1, mate, mate).wait_recv()
    fresh_move(2, cross, mate).wait_recv()
    n_new = nd * nq * new
    column = lax.broadcasted_iota(jnp.int32, (1, n_new), 1)
    block = (column % (nq * new)) // new * nd + column // (nq * new)
    goes = jnp.zeros((1, n_new), jnp.int32)
    for b in range(nd * nq):
        goes = jnp.where(block == b, owner_ref[b], goes)
    goes = goes * new + column % new - q * (nd * new)
    offset = lax.broadcasted_iota(jnp.int32, (n_keys, 1), 0) - pointer_ref[0]
    offset = jnp.where(offset < 0, offset + n_keys, offset)
    pick = jnp.where((goes == offset) & (offset < nd * new), 1.0, 0.0).astype(BF16)
    picks[...] = pick

    @pl.loop(0, width // tile)
    def _(j):
        cols = pl.ds(pl.multiple_of(j * tile, tile), tile)
        moved = jnp.dot(
            picks[...], fresh[:, :, cols].reshape(n_new, tile), preferred_element_type=F32
        )
        queue_ref[:, cols] = jnp.where(
            offset < nd * new, moved, keys[q, :, cols].astype(F32)
        ).astype(BF16)


    stores[1].start()

    def up_step(k):
        grad_side(k).wait_recv()
        part[k] += x_in[k].astype(F32)

        @pl.when(q > 0)
        def _():
            grad_up(k).wait_recv()
            part[k] += up_in[k].astype(F32)

        z_out[k] = part[k].astype(BF16)
        grad_up(k).start()

    def down_step(k):
        grad_side(k).wait_recv()
        part[k] += x_in[k].astype(F32)

        @pl.when(q < nq - 1)
        def _():
            grad_down(k).wait_recv()
            part[k] += down_in[k].astype(F32)

        z_out[k] = part[k].astype(BF16)
        grad_down(k).start()

    def own_out(h):
        return pltpu.make_async_copy(
            part.at[q * sub + h], grad_hbm.at[pl.ds(h * thin, thin)], store_sem.at[2 + h]
        )

    def own_step(k):
        grad_side(k).wait_recv()
        part[k] += x_in[k].astype(F32)

        @pl.when(q > 0)
        def _():
            grad_up(k).wait_recv()
            part[k] += up_in[k].astype(F32)

        @pl.when(q < nq - 1)
        def _():
            grad_down(k).wait_recv()
            part[k] += down_in[k].astype(F32)

    in_turn(up_step, down_step, lambda k: None)
    for h in range(sub):
        own_step(q * sub + h)
        own_out(h).start()

    def drain(k, carry):
        r = k // sub

        @pl.when((r <= q) & (q < nq - 1))
        def _():
            key_up(k).wait_send()

        @pl.when((r >= q) & (q > 0))
        def _():
            key_down(k).wait_send()

        @pl.when(r != q)
        def _():
            key_side(k).wait_send()
            key_mate(k, 0, d).wait_send()
            key_mate(k, 1, side).wait_send()

        grad_mate(k).wait_send()
        grad_side(k).wait_send()

        @pl.when(r > q)
        def _():
            grad_up(k).wait_send()

        @pl.when(r < q)
        def _():
            grad_down(k).wait_send()

        return carry

    lax.fori_loop(0, blocks, drain, 0)
    for r in range(nq):
        @pl.when(q != r)
        def _():
            fresh_out(r).wait_send()
    fresh_move(0, d, side).wait_send()
    fresh_move(1, d, mate).wait_send()
    fresh_move(2, side, mate).wait_send()
    grad_keep().wait_send()
    for store in stores:
        store.wait()
    for h in range(sub):
        own_out(h).wait()


def finish(loss_in, grad_in, queue_in, loss_out, grad_out, queue_out):
    loss_out[...] = loss_in[...]
    grad_out[...] = grad_in[...]
    queue_out[...] = queue_in[...]


def make_body(nq, nd):

    def body(
        query_inputs, key_inputs, query_weight, key_weight,
        queue_keys, write_pointer, slot_owner, positive_index,
    ):
        rows, width = query_inputs.shape
        n_keys = queue_keys.shape[0]
        new = key_inputs.shape[0]
        share = width // (nq * nd)
        sub = splits if share % (16 * splits) == 0 else 1
        blocks, thin = nq * sub, share // sub
        vmem = pl.BlockSpec(memory_space=pltpu.VMEM)
        hbm = pl.BlockSpec(memory_space=pl.ANY)
        V = pltpu.VMEM
        S = pltpu.SemaphoreType.DMA
        outs = (
            jax.ShapeDtypeStruct((1, rows), F32),
            jax.ShapeDtypeStruct((share, width), F32),
            jax.ShapeDtypeStruct((n_keys, width), BF16),
        )
        each = S((blocks,))
        made = pl.pallas_call(
            functools.partial(kernel, nq, nd),
            out_shape=outs,
            in_specs=[hbm] * 8,
            out_specs=(hbm,) * 3,
            scratch_shapes=[
                pltpu.SMEM(write_pointer.shape, jnp.int32),
                pltpu.SMEM(slot_owner.shape, jnp.int32),
                V((1, rows), jnp.int32),
                V((1, rows), F32),
                V((n_keys, width), BF16),
                V((2 * rows, n_keys), BF16),
                V((rows, 1), F32),
                V((new, width), F32),
                V((n_keys, nd * nq * new), BF16),
                V((rows, width), BF16),
                V((new, width), BF16),
                V(query_weight.shape, BF16),
                V(key_weight.shape, BF16),
                V((nq, n_keys, width), BF16),
                V((nd, nq * new, width), BF16),
                V((rows, width), F32),
                V((rows, width), BF16),
                V((rows, 1), F32),
                V((rows, 1), F32),
                V((rows, 1), F32),
                V((rows, 1), F32),
                V((rows, 1), jnp.int32),
                V((rows, width), F32),
                V((rows, width), F32),
                V((nd, nq * share, rows), BF16),
                V((rows, width), BF16),
                V((blocks, thin, width), BF16),
                V((blocks, thin, width), BF16),
                V((blocks, thin, width), BF16),
                V((blocks, thin, width), BF16),
                V((blocks, thin, width), F32),
                V((blocks, thin, width), BF16),
                V((blocks, thin, width), BF16),
                V((blocks, thin, width), BF16),
                V((blocks, thin, width), BF16),
                V((blocks, thin, width), BF16),
                S((8,)), S((2 + sub,)), each, each, each, each, each, S((blocks, 2)), S((blocks, 2)),
                S((nq,)), S((nq,)), S((3,)), S((3,)),
                each, each, S((1,)), S((1,)), each, each, each, each, each, each,
            ],
            compiler_params=pltpu.CompilerParams(
                collective_id=0, has_side_effects=True, vmem_limit_bytes=56 * 2**20
            ),
            name="contrast",
        )(
            write_pointer, slot_owner, positive_index.reshape(1, rows),
            query_inputs, key_inputs, query_weight, key_weight, queue_keys,
        )
        loss, grad, queue = pl.pallas_call(
            finish,
            out_shape=outs,
            in_specs=[vmem] * 3,
            out_specs=(vmem,) * 3,
            name="finish",
        )(*made)
        return loss.reshape(rows), grad, queue

    return body


def solution(mesh):
    in_specs = (
        P(("groups", "queue", "dp"), None),
        P(("groups", "queue", "dp"), None),
        P(),
        P(),
        P(("groups", "queue"), None),
        P("groups"),
        P("groups"),
        P(("groups", "queue", "dp")),
    )
    out_specs = (
        P(("groups", "queue", "dp")),
        P(("groups", "queue", "dp"), None),
        P(("groups", "queue"), None),
    )
    body = make_body(mesh.shape["queue"], mesh.shape["dp"])
    return jax.shard_map(body, mesh=mesh, in_specs=in_specs, out_specs=out_specs, check_vma=False)
```

```python
import functools

import jax
import jax.numpy as jnp
from jax import lax
from jax.experimental import pallas as pl
from jax.experimental.pallas import tpu as pltpu
from jax.sharding import PartitionSpec as P

temper = 0.05
splits = 2
tile = 512
strip = 32
MESH = pl.DeviceIdType.MESH
F32 = jnp.float32
BF16 = jnp.bfloat16


def dot(a, b, da, db):
    return lax.dot_general(a, b, (((da,), (db,)), ((), ())), preferred_element_type=F32)


def kernel(
    nq, nd,
    pointer_hbm, owner_hbm, index_hbm, x_hbm, kin_hbm, wq_hbm, wk_hbm, keys_hbm,
    loss_hbm, grad_hbm, queue_hbm,
    pointer_ref, owner_ref, index_ref, loss_ref, queue_ref, pair, fade, made_f, picks,
    x_ref, kin_ref, wq_ref, wk_ref, keys, fresh,
    unit_f, unit, inv_len, top, total, posit, pos_col, mixture, chosen,
    xt, grad_q, core_out, core_in, keep_out, keep_in, part, x_out, x_in, z_in, z_out,
    load_sem, store_sem, up_send, z_recv, x_send, x_recv, c_send, c_recv,
    fz_send, fz_recv, f_send, f_recv,
    gc_send, gc_recv, gk_send, gk_recv, gx_send, gx_recv, gu_send, gu_recv,
):
    q = lax.axis_index("queue")
    d = lax.axis_index("dp")
    hi, lo = d // 2, d % 2
    side = (1 - hi) * 2 + lo
    mate = hi * 2 + (1 - lo)
    cross = (1 - hi) * 2 + (1 - lo)
    rows, width = x_ref.shape
    n_keys = keys.shape[1]
    quarter = n_keys // nd
    new = kin_ref.shape[0]
    blocks = part.shape[0]
    sub = blocks // nq
    share = grad_hbm.shape[0]
    thin = share // sub
    cut = quarter // sub
    micro = (nq - 1) * sub

    loads = [
        pltpu.make_async_copy(src, dst, load_sem.at[i])
        for i, (src, dst) in enumerate(
            (
                (x_hbm, x_ref),
                (wq_hbm, wq_ref),
                (keys_hbm, keys.at[q]),
                (kin_hbm, kin_ref),
                (wk_hbm, wk_ref),
                (index_hbm, index_ref),
                (owner_hbm, owner_ref),
                (pointer_hbm, pointer_ref),
            )
        )
    ]
    for load in loads:
        load.start()

    def piece(k, part_of):
        start = part_of * quarter + lax.rem(k, sub) * cut
        return keys.at[k // sub, pl.ds(pl.multiple_of(start, cut), cut)]

    def remote(src, dst, send, recv, where):
        return pltpu.make_async_remote_copy(
            src_ref=src, dst_ref=dst, send_sem=send, recv_sem=recv,
            device_id=where, device_id_type=MESH,
        )

    def own_piece(h):
        return keys_hbm.at[pl.ds(pl.multiple_of(d * quarter + h * cut, cut), cut)]

    def key_out(r, h):
        return remote(
            own_piece(h), piece(q * sub + h, d), up_send.at[r * sub + h], z_recv.at[q * sub + h],
            {"queue": r},
        )

    def key_in(k):
        return remote(piece(k, d), piece(k, d), up_send.at[k], z_recv.at[k], {"queue": k // sub})

    def key_side(k):
        return remote(piece(k, d), piece(k, d), x_send.at[k], x_recv.at[k], {"dp": side})

    def key_side_in(k):
        return remote(piece(k, side), piece(k, side), x_send.at[k], x_recv.at[k], {"dp": side})

    def key_mate(k, i, part_of):
        return remote(piece(k, part_of), piece(k, part_of), c_send.at[k, i], c_recv.at[k, i], {"dp": mate})

    barrier = pltpu.get_barrier_semaphore()
    pl.semaphore_signal(barrier, inc=1, device_id={"dp": side}, device_id_type=MESH)
    pl.semaphore_signal(barrier, inc=1, device_id={"dp": mate}, device_id_type=MESH)
    for r in range(nq):
        @pl.when(q != r)
        def _():
            pl.semaphore_signal(barrier, inc=1, device_id={"queue": r}, device_id_type=MESH)
    pl.semaphore_wait(barrier, nq + 1)

    def others(m, act):
        s, h = m // sub + 1, lax.rem(m, sub)

        @pl.when(q - s >= 0)
        def _():
            act(q - s, h)

        @pl.when(q + s <= nq - 1)
        def _():
            act(q + s, h)

    @pl.loop(0, micro)
    def _(m):
        others(m, lambda r, h: key_out(r, h).start())

    loads[0].wait()
    loads[1].wait()
    inv_len[...] = jnp.zeros(inv_len.shape, F32)

    @pl.loop(0, width // tile)
    def _(j):
        cols = pl.ds(pl.multiple_of(j * tile, tile), tile)
        query = jnp.dot(x_ref[...], wq_ref[:, cols], preferred_element_type=F32)
        unit_f[:, cols] = query
        inv_len[...] += jnp.sum(query * query, -1, keepdims=True)

    inv_len[...] = lax.rsqrt(inv_len[...] + 1e-06)

    @pl.loop(0, rows // strip)
    def _(i):
        at = pl.ds(pl.multiple_of(i * strip, strip), strip)
        query = unit_f[at] * inv_len[at]
        unit_f[at] = query
        unit[at] = query.astype(BF16)
        mixture[at] = jnp.zeros((strip, width), F32)
        chosen[at] = jnp.zeros((strip, width), F32)

    top[...] = jnp.full(top.shape, -1e30, F32)
    total[...] = jnp.zeros(total.shape, F32)
    posit[...] = jnp.zeros(posit.shape, F32)
    eye = lax.broadcasted_iota(jnp.int32, (rows, rows), 0) == lax.broadcasted_iota(
        jnp.int32, (rows, rows), 1
    )
    loads[5].wait()
    pos_col[...] = jnp.sum(jnp.where(eye, index_ref[...], 0), -1, keepdims=True)

    def fold(r):
        block = keys[r]
        scores = dot(unit[...], block, 1, 1) / temper
        hit = lax.broadcasted_iota(jnp.int32, (rows, n_keys), 1) + r * n_keys == pos_col[...]
        posit[...] += jnp.sum(jnp.where(hit, scores, 0.0), -1, keepdims=True)
        old = top[...]
        high = jnp.maximum(old, jnp.max(scores, -1, keepdims=True))
        decay = jnp.exp(old - high)
        expo = jnp.exp(scores - high)
        top[...] = high
        total[...] = total[...] * decay + jnp.sum(expo, -1, keepdims=True)
        pair[:rows] = expo.astype(BF16)
        pair[rows:] = jnp.where(hit, 1.0, 0.0).astype(BF16)
        fade[...] = decay

        @pl.loop(0, width // tile)
        def _(j):
            cols = pl.ds(pl.multiple_of(j * tile, tile), tile)
            both = jnp.dot(pair[...], keys[r, :, cols], preferred_element_type=F32)
            mixture[:, cols] = mixture[:, cols] * fade[...] + both[:rows]
            chosen[:, cols] += both[rows:]


    def make_fresh():
        loads[3].wait()
        loads[4].wait()

        @pl.loop(0, width // tile)
        def _(j):
            cols = pl.ds(pl.multiple_of(j * tile, tile), tile)
            made_f[:, cols] = jnp.dot(kin_ref[...], wk_ref[:, cols], preferred_element_type=F32)

        made = made_f[...]
        made = (made * lax.rsqrt(jnp.sum(made * made, -1, keepdims=True) + 1e-06)).astype(BF16)
        fresh[d, pl.ds(pl.multiple_of(q * new, new), new)] = made

    def fresh_out(r):
        slot = fresh.at[d, pl.ds(pl.multiple_of(q * new, new), new)]
        return remote(slot, slot, fz_send.at[r], fz_recv.at[q], {"queue": r})

    def fresh_in(r):
        slot = fresh.at[d, pl.ds(pl.multiple_of(r * new, new), new)]
        return remote(slot, slot, fz_send.at[r], fz_recv.at[r], {"queue": r})

    def fresh_move(k, part_of, where):
        return remote(fresh.at[part_of], fresh.at[part_of], f_send.at[k], f_recv.at[k], {"dp": where})

    def turn():
        if nd * share % 128 == 0:
            @pl.loop(0, nq)
            def _(r):
                cols = pl.ds(pl.multiple_of(r * nd * share, nd * share), nd * share)
                turned = x_ref[:, cols].astype(F32).T.astype(BF16)
                for p in range(nd):
                    xt[p, pl.ds(pl.multiple_of(r * share, share), share)] = turned[p * share : (p + 1) * share]

            return
        turned = x_ref[...].astype(F32).T
        for p in range(nd):
            xt[p] = jnp.concatenate(
                [turned[(r * nd + p) * share : (r * nd + p + 1) * share] for r in range(nq)], axis=0
            ).astype(BF16)

    loads[2].wait()
    fold(q)

    def pass_on(r, h):
        k = r * sub + h
        key_in(k).wait_recv()
        key_side(k).start()
        key_mate(k, 0, d).start()

    def pass_side(r, h):
        k = r * sub + h
        key_side_in(k).wait_recv()
        key_mate(k, 1, side).start()

    def step(m, carry):
        @pl.when(m < micro)
        def _():
            others(m, pass_on)

        @pl.when(m == 0)
        def _():
            make_fresh()

        @pl.when(m == 1)
        def _():
            turn()

        @pl.when(m == micro - 1)
        def _():
            for r in range(nq):
                @pl.when(q != r)
                def _():
                    fresh_out(r).start()

        @pl.when((m >= 2) & (m < micro + 2))
        def _():
            others(m - 2, pass_side)

        def both(i, carry):
            r = q + ((m - 3) // sub + 1) * (2 * i - 1)
            later = (m >= 3) & (lax.rem(m, sub) == 2 % sub) & (r >= 0) & (r <= nq - 1)

            @pl.when(later)
            def _():
                for h in range(sub):
                    key_mate(r * sub + h, 0, mate).wait_recv()
                    key_mate(r * sub + h, 1, cross).wait_recv()
                fold(r)

            return carry

        lax.fori_loop(0, 2, both, 0)

        return carry

    lax.fori_loop(0, micro + 3, step, 0)

    for r in range(nq):
        @pl.when(q != r)
        def _():
            fresh_in(r).wait_recv()
    fresh_move(0, d, side).start()
    fresh_move(1, d, mate).start()

    @pl.loop(0, rows // strip)
    def _(i):
        at = pl.ds(pl.multiple_of(i * strip, strip), strip)
        grad_unit = mixture[at] * (1.0 / (total[at] * temper)) - chosen[at] * (1.0 / temper)
        units = unit_f[at]
        grad_q[at] = (
            (grad_unit - units * jnp.sum(units * grad_unit, -1, keepdims=True)) * inv_len[at]
        ).astype(BF16)

    def term(p, out):
        @pl.loop(0, width // tile)
        def _(j):
            cols = pl.ds(pl.multiple_of(j * tile, tile), tile)
            got = jnp.dot(xt[p], grad_q[:, cols], preferred_element_type=F32)
            out[:, :, cols] = got.reshape(blocks, thin, tile).astype(out.dtype)

    def grad_mate(k):
        return remote(core_out.at[k], core_in.at[k], gc_send.at[k], gc_recv.at[k], {"dp": mate})

    def grad_keep():
        return remote(keep_out, keep_in, gk_send.at[0], gk_recv.at[0], {"dp": mate})

    def grad_side(k):
        return remote(x_out.at[k], x_in.at[k], gx_send.at[k], gx_recv.at[k], {"dp": side})

    def grad_out(r, h):
        return remote(
            z_out.at[r * sub + h], z_in.at[q * sub + h], gu_send.at[r * sub + h],
            gu_recv.at[q * sub + h], {"queue": r},
        )

    def grad_in(k):
        return remote(z_out.at[k], z_in.at[k], gu_send.at[k], gu_recv.at[k], {"queue": k // sub})

    def in_turn(act, own=True):
        @pl.loop(0, micro)
        def _(m):
            back = (nq - 2 - m // sub) * sub + lax.rem(m, sub)
            others(back, act)

        if own:
            @pl.loop(0, sub)
            def _(h):
                act(q, h)

    def start_mate(r, h):
        grad_mate(r * sub + h).start()

    term(cross, core_out)
    in_turn(start_mate)
    term(side, part)
    term(mate, keep_out)
    grad_keep().start()

    def start_side(r, h):
        k = r * sub + h
        grad_mate(k).wait_recv()
        x_out[k] = (part[k] + core_in[k].astype(F32)).astype(BF16)
        grad_side(k).start()

    in_turn(start_side)
    fresh_move(0, side, side).wait_recv()
    fresh_move(2, side, mate).start()
    term(d, part)
    grad_keep().wait_recv()

    @pl.loop(0, blocks)
    def _(k):
        part[k] += keep_in[k].astype(F32)

    loss_col = top[...] + jnp.log(total[...]) - posit[...]
    loss_ref[...] = jnp.sum(jnp.where(eye, loss_col, 0.0), 0, keepdims=True)
    stores = [
        pltpu.make_async_copy(loss_ref, loss_hbm, store_sem.at[0]),
        pltpu.make_async_copy(queue_ref, queue_hbm, store_sem.at[1]),
    ]
    stores[0].start()

    loads[6].wait()
    loads[7].wait()
    fresh_move(1, mate, mate).wait_recv()
    fresh_move(2, cross, mate).wait_recv()
    n_new = nd * nq * new
    column = lax.broadcasted_iota(jnp.int32, (1, n_new), 1)
    block = (column % (nq * new)) // new * nd + column // (nq * new)
    goes = jnp.zeros((1, n_new), jnp.int32)
    for b in range(nd * nq):
        goes = jnp.where(block == b, owner_ref[b], goes)
    goes = goes * new + column % new - q * (nd * new)
    offset = lax.broadcasted_iota(jnp.int32, (n_keys, 1), 0) - pointer_ref[0]
    offset = jnp.where(offset < 0, offset + n_keys, offset)
    pick = jnp.where((goes == offset) & (offset < nd * new), 1.0, 0.0).astype(BF16)
    picks[...] = pick

    @pl.loop(0, width // tile)
    def _(j):
        cols = pl.ds(pl.multiple_of(j * tile, tile), tile)
        moved = jnp.dot(
            picks[...], fresh[:, :, cols].reshape(n_new, tile), preferred_element_type=F32
        )
        queue_ref[:, cols] = jnp.where(
            offset < nd * new, moved, keys[q, :, cols].astype(F32)
        ).astype(BF16)


    stores[1].start()

    def send_on(r, h):
        k = r * sub + h
        grad_side(k).wait_recv()
        z_out[k] = (part[k] + x_in[k].astype(F32)).astype(BF16)
        grad_out(r, h).start()

    def own_out(h):
        return pltpu.make_async_copy(
            part.at[q * sub + h], grad_hbm.at[pl.ds(h * thin, thin)], store_sem.at[2 + h]
        )

    in_turn(send_on, own=False)

    def own_step(h):
        mine = q * sub + h
        grad_side(mine).wait_recv()
        part[mine] += x_in[mine].astype(F32)

        def add(r, carry):
            @pl.when(r != q)
            def _():
                grad_in(r * sub + h).wait_recv()
                part[mine] += z_in[r * sub + h].astype(F32)

            return carry

        lax.fori_loop(0, nq, add, 0)
        own_out(h).start()

    for h in range(sub):
        own_step(h)

    def drain(k, carry):
        r = k // sub

        @pl.when(r != q)
        def _():
            key_out(r, lax.rem(k, sub)).wait_send()
            key_side(k).wait_send()
            key_mate(k, 0, d).wait_send()
            key_mate(k, 1, side).wait_send()
            grad_out(r, lax.rem(k, sub)).wait_send()

        grad_mate(k).wait_send()
        grad_side(k).wait_send()
        return carry

    lax.fori_loop(0, blocks, drain, 0)
    for r in range(nq):
        @pl.when(q != r)
        def _():
            fresh_out(r).wait_send()
    fresh_move(0, d, side).wait_send()
    fresh_move(1, d, mate).wait_send()
    fresh_move(2, side, mate).wait_send()
    grad_keep().wait_send()
    for store in stores:
        store.wait()
    for h in range(sub):
        own_out(h).wait()


def finish(loss_in, grad_in, queue_in, loss_out, grad_out, queue_out):
    loss_out[...] = loss_in[...]
    grad_out[...] = grad_in[...]
    queue_out[...] = queue_in[...]


def make_body(nq, nd):

    def body(
        query_inputs, key_inputs, query_weight, key_weight,
        queue_keys, write_pointer, slot_owner, positive_index,
    ):
        rows, width = query_inputs.shape
        n_keys = queue_keys.shape[0]
        new = key_inputs.shape[0]
        share = width // (nq * nd)
        sub = splits if share % (16 * splits) == 0 else 1
        blocks, thin = nq * sub, share // sub
        vmem = pl.BlockSpec(memory_space=pltpu.VMEM)
        hbm = pl.BlockSpec(memory_space=pl.ANY)
        V = pltpu.VMEM
        S = pltpu.SemaphoreType.DMA
        outs = (
            jax.ShapeDtypeStruct((1, rows), F32),
            jax.ShapeDtypeStruct((share, width), F32),
            jax.ShapeDtypeStruct((n_keys, width), BF16),
        )
        each = S((blocks,))
        made = pl.pallas_call(
            functools.partial(kernel, nq, nd),
            out_shape=outs,
            in_specs=[hbm] * 8,
            out_specs=(hbm,) * 3,
            scratch_shapes=[
                pltpu.SMEM(write_pointer.shape, jnp.int32),
                pltpu.SMEM(slot_owner.shape, jnp.int32),
                V((1, rows), jnp.int32),
                V((1, rows), F32),
                V((n_keys, width), BF16),
                V((2 * rows, n_keys), BF16),
                V((rows, 1), F32),
                V((new, width), F32),
                V((n_keys, nd * nq * new), BF16),
                V((rows, width), BF16),
                V((new, width), BF16),
                V(query_weight.shape, BF16),
                V(key_weight.shape, BF16),
                V((nq, n_keys, width), BF16),
                V((nd, nq * new, width), BF16),
                V((rows, width), F32),
                V((rows, width), BF16),
                V((rows, 1), F32),
                V((rows, 1), F32),
                V((rows, 1), F32),
                V((rows, 1), F32),
                V((rows, 1), jnp.int32),
                V((rows, width), F32),
                V((rows, width), F32),
                V((nd, nq * share, rows), BF16),
                V((rows, width), BF16),
                V((blocks, thin, width), BF16),
                V((blocks, thin, width), BF16),
                V((blocks, thin, width), BF16),
                V((blocks, thin, width), BF16),
                V((blocks, thin, width), F32),
                V((blocks, thin, width), BF16),
                V((blocks, thin, width), BF16),
                V((blocks, thin, width), BF16),
                V((blocks, thin, width), BF16),
                S((8,)), S((2 + sub,)), each, each, each, each, S((blocks, 2)), S((blocks, 2)),
                S((nq,)), S((nq,)), S((3,)), S((3,)),
                each, each, S((1,)), S((1,)), each, each, each, each,
            ],
            compiler_params=pltpu.CompilerParams(
                collective_id=0, has_side_effects=True, vmem_limit_bytes=56 * 2**20
            ),
            name="contrast",
        )(
            write_pointer, slot_owner, positive_index.reshape(1, rows),
            query_inputs, key_inputs, query_weight, key_weight, queue_keys,
        )
        loss, grad, queue = pl.pallas_call(
            finish,
            out_shape=outs,
            in_specs=[vmem] * 3,
            out_specs=(vmem,) * 3,
            name="finish",
        )(*made)
        return loss.reshape(rows), grad, queue

    return body


def solution(mesh):
    in_specs = (
        P(("groups", "queue", "dp"), None),
        P(("groups", "queue", "dp"), None),
        P(),
        P(),
        P(("groups", "queue"), None),
        P("groups"),
        P("groups"),
        P(("groups", "queue", "dp")),
    )
    out_specs = (
        P(("groups", "queue", "dp")),
        P(("groups", "queue", "dp"), None),
        P(("groups", "queue"), None),
    )
    body = make_body(mesh.shape["queue"], mesh.shape["dp"])
    return jax.shard_map(body, mesh=mesh, in_specs=in_specs, out_specs=out_specs, check_vma=False)
```

```python
import functools

import jax
import jax.numpy as jnp
from jax import lax
from jax.experimental import pallas as pl
from jax.experimental.pallas import tpu as pltpu
from jax.sharding import PartitionSpec as P

temper = 0.05
splits = 2
MESH = pl.DeviceIdType.MESH
F32 = jnp.float32
BF16 = jnp.bfloat16


def dot(a, b, da, db):
    return lax.dot_general(a, b, (((da,), (db,)), ((), ())), preferred_element_type=F32)


def kernel(
    nq, nd,
    pointer_hbm, owner_hbm, index_hbm, x_hbm, kin_hbm, wq_hbm, wk_hbm, keys_hbm,
    loss_hbm, grad_hbm, queue_hbm,
    pointer_ref, owner_ref, index_ref, loss_ref, queue_ref,
    x_ref, kin_ref, wq_ref, wk_ref, keys, fresh,
    unit_f, unit, inv_len, top, total, posit, pos_col, mixture, chosen,
    xt, grad_q, core_out, core_in, keep_out, keep_in, part, x_out, x_in, up_in, down_in, z_out,
    load_sem, store_sem, up_send, down_send, z_recv, x_send, x_recv, c_send, c_recv,
    fz_send, fz_recv, f_send, f_recv,
    gc_send, gc_recv, gk_send, gk_recv, gx_send, gx_recv, gu_send, gd_send, gu_recv, gd_recv,
):
    q = lax.axis_index("queue")
    d = lax.axis_index("dp")
    hi, lo = d // 2, d % 2
    side = (1 - hi) * 2 + lo
    mate = hi * 2 + (1 - lo)
    cross = (1 - hi) * 2 + (1 - lo)
    rows, width = x_ref.shape
    n_keys = keys.shape[1]
    quarter = n_keys // nd
    new = kin_ref.shape[0]
    blocks = part.shape[0]
    sub = blocks // nq
    share = grad_hbm.shape[0]
    thin = share // sub
    cut = quarter // sub
    micro = (nq - 1) * sub

    loads = [
        pltpu.make_async_copy(src, dst, load_sem.at[i])
        for i, (src, dst) in enumerate(
            (
                (x_hbm, x_ref),
                (wq_hbm, wq_ref),
                (keys_hbm, keys.at[q]),
                (kin_hbm, kin_ref),
                (wk_hbm, wk_ref),
                (index_hbm, index_ref),
                (owner_hbm, owner_ref),
                (pointer_hbm, pointer_ref),
            )
        )
    ]
    for load in loads:
        load.start()

    def piece(k, part_of):
        start = part_of * quarter + lax.rem(k, sub) * cut
        return keys.at[k // sub, pl.ds(pl.multiple_of(start, cut), cut)]

    def remote(src, dst, send, recv, where):
        return pltpu.make_async_remote_copy(
            src_ref=src, dst_ref=dst, send_sem=send, recv_sem=recv,
            device_id=where, device_id_type=MESH,
        )

    above = {"queue": jnp.minimum(q + 1, nq - 1)}
    below = {"queue": jnp.maximum(q - 1, 0)}

    def own_piece(h):
        return keys_hbm.at[pl.ds(pl.multiple_of(d * quarter + h * cut, cut), cut)]

    def key_up(k, src=None):
        src = piece(k, d) if src is None else src
        return remote(src, piece(k, d), up_send.at[k], z_recv.at[k], above)

    def key_down(k, src=None):
        src = piece(k, d) if src is None else src
        return remote(src, piece(k, d), down_send.at[k], z_recv.at[k], below)

    def key_side(k):
        return remote(piece(k, d), piece(k, d), x_send.at[k], x_recv.at[k], {"dp": side})

    def key_side_in(k):
        return remote(piece(k, side), piece(k, side), x_send.at[k], x_recv.at[k], {"dp": side})

    def key_mate(k, i, part_of):
        return remote(piece(k, part_of), piece(k, part_of), c_send.at[k, i], c_recv.at[k, i], {"dp": mate})

    barrier = pltpu.get_barrier_semaphore()
    pl.semaphore_signal(barrier, inc=1, device_id={"dp": side}, device_id_type=MESH)
    pl.semaphore_signal(barrier, inc=1, device_id={"dp": mate}, device_id_type=MESH)
    for r in range(nq):
        @pl.when(q != r)
        def _():
            pl.semaphore_signal(barrier, inc=1, device_id={"queue": r}, device_id_type=MESH)
    pl.semaphore_wait(barrier, nq + 1)

    for h in range(sub):
        @pl.when(q < nq - 1)
        def _():
            key_up(q * sub + h, own_piece(h)).start()

        @pl.when(q > 0)
        def _():
            key_down(q * sub + h, own_piece(h)).start()

    loads[0].wait()
    loads[1].wait()
    query = jnp.dot(x_ref[...], wq_ref[...], preferred_element_type=F32)
    scale = lax.rsqrt(jnp.sum(query * query, -1, keepdims=True) + 1e-06)
    inv_len[...] = scale
    query = query * scale
    unit_f[...] = query
    unit[...] = query.astype(BF16)
    top[...] = jnp.full(top.shape, -1e30, F32)
    total[...] = jnp.zeros(total.shape, F32)
    posit[...] = jnp.zeros(posit.shape, F32)
    mixture[...] = jnp.zeros(mixture.shape, F32)
    chosen[...] = jnp.zeros(chosen.shape, F32)
    eye = lax.broadcasted_iota(jnp.int32, (rows, rows), 0) == lax.broadcasted_iota(
        jnp.int32, (rows, rows), 1
    )
    loads[5].wait()
    pos_col[...] = jnp.sum(jnp.where(eye, index_ref[...], 0), -1, keepdims=True)

    def fold(r):
        block = keys[r]
        scores = dot(unit[...], block, 1, 1) / temper
        hit = lax.broadcasted_iota(jnp.int32, (rows, n_keys), 1) + r * n_keys == pos_col[...]
        posit[...] += jnp.sum(jnp.where(hit, scores, 0.0), -1, keepdims=True)
        old = top[...]
        high = jnp.maximum(old, jnp.max(scores, -1, keepdims=True))
        decay = jnp.exp(old - high)
        expo = jnp.exp(scores - high)
        top[...] = high
        total[...] = total[...] * decay + jnp.sum(expo, -1, keepdims=True)
        mixture[...] = mixture[...] * decay + jnp.dot(
            expo.astype(BF16), block, preferred_element_type=F32
        )
        chosen[...] += jnp.dot(
            jnp.where(hit, 1.0, 0.0).astype(BF16), block, preferred_element_type=F32
        )

    def make_fresh():
        loads[3].wait()
        loads[4].wait()
        made = jnp.dot(kin_ref[...], wk_ref[...], preferred_element_type=F32)
        made = (made * lax.rsqrt(jnp.sum(made * made, -1, keepdims=True) + 1e-06)).astype(BF16)
        fresh[d, pl.ds(pl.multiple_of(q * new, new), new)] = made

    def fresh_out(r):
        slot = fresh.at[d, pl.ds(pl.multiple_of(q * new, new), new)]
        return remote(slot, slot, fz_send.at[r], fz_recv.at[q], {"queue": r})

    def fresh_in(r):
        slot = fresh.at[d, pl.ds(pl.multiple_of(r * new, new), new)]
        return remote(slot, slot, fz_send.at[r], fz_recv.at[r], {"queue": r})

    def fresh_move(k, part_of, where):
        return remote(fresh.at[part_of], fresh.at[part_of], f_send.at[k], f_recv.at[k], {"dp": where})

    def turn():
        turned = x_ref[...].astype(F32).T
        for p in range(nd):
            xt[p] = jnp.concatenate(
                [turned[(r * nd + p) * share : (r * nd + p + 1) * share] for r in range(nq)], axis=0
            ).astype(BF16)

    def others(m, act):
        s, h = m // sub + 1, lax.rem(m, sub)

        @pl.when(q - s >= 0)
        def _():
            act((q - s) * sub + h, True)

        @pl.when(q + s <= nq - 1)
        def _():
            act((q + s) * sub + h, False)

    def pass_on(k, upward):
        key_up(k).wait_recv()
        if upward:
            @pl.when(q < nq - 1)
            def _():
                key_up(k).start()
        else:
            @pl.when(q > 0)
            def _():
                key_down(k).start()
        key_side(k).start()
        key_mate(k, 0, d).start()

    def pass_side(k, upward):
        key_side_in(k).wait_recv()
        key_mate(k, 1, side).start()

    def step(m, carry):
        @pl.when(m < micro)
        def _():
            others(m, pass_on)

        @pl.when(m == micro - 1)
        def _():
            for r in range(nq):
                @pl.when(q != r)
                def _():
                    fresh_out(r).start()

        @pl.when((m >= 2) & (m < micro + 2))
        def _():
            others(m - 2, pass_side)

        @pl.when(m == 1)
        def _():
            loads[2].wait()
            fold(q)

        @pl.when(m == 2)
        def _():
            make_fresh()

        @pl.when(m == 3)
        def _():
            turn()

        @pl.when((m >= 3) & (lax.rem(m, sub) == (sub + 2) % sub))
        def _():
            def both(i, carry):
                r = q + ((m - 3) // sub + 1) * (2 * i - 1)

                @pl.when((r >= 0) & (r <= nq - 1))
                def _():
                    for h in range(sub):
                        key_mate(r * sub + h, 0, mate).wait_recv()
                        key_mate(r * sub + h, 1, cross).wait_recv()
                    fold(r)

                return carry

            lax.fori_loop(0, 2, both, 0)

        return carry

    lax.fori_loop(0, micro + 3, step, 0)

    for r in range(nq):
        @pl.when(q != r)
        def _():
            fresh_in(r).wait_recv()
    fresh_move(0, d, side).start()
    fresh_move(1, d, mate).start()

    count = total[...]
    grad_unit = mixture[...] * (1.0 / (count * temper)) - chosen[...] * (1.0 / temper)
    units = unit_f[...]
    grad_q[...] = (
        (grad_unit - units * jnp.sum(units * grad_unit, -1, keepdims=True)) * inv_len[...]
    ).astype(BF16)

    def term(p):
        return jnp.dot(xt[p], grad_q[...], preferred_element_type=F32).reshape(blocks, thin, width)

    def grad_mate(k):
        return remote(core_out.at[k], core_in.at[k], gc_send.at[k], gc_recv.at[k], {"dp": mate})

    def grad_keep():
        return remote(keep_out, keep_in, gk_send.at[0], gk_recv.at[0], {"dp": mate})

    def grad_side(k):
        return remote(x_out.at[k], x_in.at[k], gx_send.at[k], gx_recv.at[k], {"dp": side})

    def grad_up(k):
        return remote(z_out.at[k], up_in.at[k], gu_send.at[k], gu_recv.at[k], above)

    def grad_down(k):
        return remote(z_out.at[k], down_in.at[k], gd_send.at[k], gd_recv.at[k], below)

    def in_turn(act_up, act_down, act_own):
        def at(t, carry):
            for_up = nq - 1 - (t - q)
            for_down = t - (nq - 1 - q)
            for h in range(sub):
                @pl.when((t >= q) & (for_up > q))
                def _():
                    act_up(for_up * sub + h)

                @pl.when((for_down >= 0) & (for_down < q))
                def _():
                    act_down(for_down * sub + h)

            return carry

        lax.fori_loop(0, nq - 1, at, 0)
        for h in range(sub):
            act_own(q * sub + h)

    def start_mate(k):
        grad_mate(k).start()

    core_out[...] = term(cross).astype(BF16)
    in_turn(start_mate, start_mate, start_mate)
    part[...] = term(side)
    keep_out[...] = term(mate).astype(BF16)
    grad_keep().start()

    def start_side(k):
        grad_mate(k).wait_recv()
        x_out[k] = (part[k] + core_in[k].astype(F32)).astype(BF16)
        grad_side(k).start()

    in_turn(start_side, start_side, start_side)
    fresh_move(0, side, side).wait_recv()
    fresh_move(2, side, mate).start()
    part[...] = term(d)
    grad_keep().wait_recv()
    part[...] += keep_in[...].astype(F32)

    loss_col = top[...] + jnp.log(count) - posit[...]
    loss_ref[...] = jnp.sum(jnp.where(eye, loss_col, 0.0), 0, keepdims=True)
    stores = [
        pltpu.make_async_copy(loss_ref, loss_hbm, store_sem.at[0]),
        pltpu.make_async_copy(queue_ref, queue_hbm, store_sem.at[1]),
    ]
    stores[0].start()

    loads[6].wait()
    loads[7].wait()
    fresh_move(1, mate, mate).wait_recv()
    fresh_move(2, cross, mate).wait_recv()
    n_new = nd * nq * new
    column = lax.broadcasted_iota(jnp.int32, (1, n_new), 1)
    block = (column % (nq * new)) // new * nd + column // (nq * new)
    goes = jnp.zeros((1, n_new), jnp.int32)
    for b in range(nd * nq):
        goes = jnp.where(block == b, owner_ref[b], goes)
    goes = goes * new + column % new - q * (nd * new)
    offset = lax.broadcasted_iota(jnp.int32, (n_keys, 1), 0) - pointer_ref[0]
    offset = jnp.where(offset < 0, offset + n_keys, offset)
    pick = jnp.where((goes == offset) & (offset < nd * new), 1.0, 0.0).astype(BF16)
    moved = jnp.dot(pick, fresh[...].reshape(n_new, width), preferred_element_type=F32)
    queue_ref[...] = jnp.where(offset < nd * new, moved, keys[q].astype(F32)).astype(BF16)

    stores[1].start()

    def up_step(k):
        grad_side(k).wait_recv()
        part[k] += x_in[k].astype(F32)

        @pl.when(q > 0)
        def _():
            grad_up(k).wait_recv()
            part[k] += up_in[k].astype(F32)

        z_out[k] = part[k].astype(BF16)
        grad_up(k).start()

    def down_step(k):
        grad_side(k).wait_recv()
        part[k] += x_in[k].astype(F32)

        @pl.when(q < nq - 1)
        def _():
            grad_down(k).wait_recv()
            part[k] += down_in[k].astype(F32)

        z_out[k] = part[k].astype(BF16)
        grad_down(k).start()

    def own_out(h):
        return pltpu.make_async_copy(
            part.at[q * sub + h], grad_hbm.at[pl.ds(h * thin, thin)], store_sem.at[2 + h]
        )

    def own_step(k):
        grad_side(k).wait_recv()
        part[k] += x_in[k].astype(F32)

        @pl.when(q > 0)
        def _():
            grad_up(k).wait_recv()
            part[k] += up_in[k].astype(F32)

        @pl.when(q < nq - 1)
        def _():
            grad_down(k).wait_recv()
            part[k] += down_in[k].astype(F32)

    in_turn(up_step, down_step, lambda k: None)
    for h in range(sub):
        own_step(q * sub + h)
        own_out(h).start()

    def drain(k, carry):
        r = k // sub

        @pl.when((r <= q) & (q < nq - 1))
        def _():
            key_up(k).wait_send()

        @pl.when((r >= q) & (q > 0))
        def _():
            key_down(k).wait_send()

        @pl.when(r != q)
        def _():
            key_side(k).wait_send()
            key_mate(k, 0, d).wait_send()
            key_mate(k, 1, side).wait_send()

        grad_mate(k).wait_send()
        grad_side(k).wait_send()

        @pl.when(r > q)
        def _():
            grad_up(k).wait_send()

        @pl.when(r < q)
        def _():
            grad_down(k).wait_send()

        return carry

    lax.fori_loop(0, blocks, drain, 0)
    for r in range(nq):
        @pl.when(q != r)
        def _():
            fresh_out(r).wait_send()
    fresh_move(0, d, side).wait_send()
    fresh_move(1, d, mate).wait_send()
    fresh_move(2, side, mate).wait_send()
    grad_keep().wait_send()
    for store in stores:
        store.wait()
    for h in range(sub):
        own_out(h).wait()


def finish(loss_in, grad_in, queue_in, loss_out, grad_out, queue_out):
    loss_out[...] = loss_in[...]
    grad_out[...] = grad_in[...]
    queue_out[...] = queue_in[...]


def make_body(nq, nd):

    def body(
        query_inputs, key_inputs, query_weight, key_weight,
        queue_keys, write_pointer, slot_owner, positive_index,
    ):
        rows, width = query_inputs.shape
        n_keys = queue_keys.shape[0]
        new = key_inputs.shape[0]
        share = width // (nq * nd)
        sub = splits if share % (16 * splits) == 0 else 1
        blocks, thin = nq * sub, share // sub
        vmem = pl.BlockSpec(memory_space=pltpu.VMEM)
        hbm = pl.BlockSpec(memory_space=pl.ANY)
        V = pltpu.VMEM
        S = pltpu.SemaphoreType.DMA
        outs = (
            jax.ShapeDtypeStruct((1, rows), F32),
            jax.ShapeDtypeStruct((share, width), F32),
            jax.ShapeDtypeStruct((n_keys, width), BF16),
        )
        each = S((blocks,))
        made = pl.pallas_call(
            functools.partial(kernel, nq, nd),
            out_shape=outs,
            in_specs=[hbm] * 8,
            out_specs=(hbm,) * 3,
            scratch_shapes=[
                pltpu.SMEM(write_pointer.shape, jnp.int32),
                pltpu.SMEM(slot_owner.shape, jnp.int32),
                V((1, rows), jnp.int32),
                V((1, rows), F32),
                V((n_keys, width), BF16),
                V((rows, width), BF16),
                V((new, width), BF16),
                V(query_weight.shape, BF16),
                V(key_weight.shape, BF16),
                V((nq, n_keys, width), BF16),
                V((nd, nq * new, width), BF16),
                V((rows, width), F32),
                V((rows, width), BF16),
                V((rows, 1), F32),
                V((rows, 1), F32),
                V((rows, 1), F32),
                V((rows, 1), F32),
                V((rows, 1), jnp.int32),
                V((rows, width), F32),
                V((rows, width), F32),
                V((nd, nq * share, rows), BF16),
                V((rows, width), BF16),
                V((blocks, thin, width), BF16),
                V((blocks, thin, width), BF16),
                V((blocks, thin, width), BF16),
                V((blocks, thin, width), BF16),
                V((blocks, thin, width), F32),
                V((blocks, thin, width), BF16),
                V((blocks, thin, width), BF16),
                V((blocks, thin, width), BF16),
                V((blocks, thin, width), BF16),
                V((blocks, thin, width), BF16),
                S((8,)), S((2 + sub,)), each, each, each, each, each, S((blocks, 2)), S((blocks, 2)),
                S((nq,)), S((nq,)), S((3,)), S((3,)),
                each, each, S((1,)), S((1,)), each, each, each, each, each, each,
            ],
            compiler_params=pltpu.CompilerParams(
                collective_id=0, has_side_effects=True, vmem_limit_bytes=56 * 2**20
            ),
            name="contrast",
        )(
            write_pointer, slot_owner, positive_index.reshape(1, rows),
            query_inputs, key_inputs, query_weight, key_weight, queue_keys,
        )
        loss, grad, queue = pl.pallas_call(
            finish,
            out_shape=outs,
            in_specs=[vmem] * 3,
            out_specs=(vmem,) * 3,
            name="finish",
        )(*made)
        return loss.reshape(rows), grad, queue

    return body


def solution(mesh):
    in_specs = (
        P(("groups", "queue", "dp"), None),
        P(("groups", "queue", "dp"), None),
        P(),
        P(),
        P(("groups", "queue"), None),
        P("groups"),
        P("groups"),
        P(("groups", "queue", "dp")),
    )
    out_specs = (
        P(("groups", "queue", "dp")),
        P(("groups", "queue", "dp"), None),
        P(("groups", "queue"), None),
    )
    body = make_body(mesh.shape["queue"], mesh.shape["dp"])
    return jax.shard_map(body, mesh=mesh, in_specs=in_specs, out_specs=out_specs, check_vma=False)
```
